128 devices in a mesh: grp: 8 (over x, core), sib: 16 (over y, z).
Axes of the slice: x: 4, y: 4, z: 4, core: 2. Of those that a mesh axis runs over, the one named last changes fastest.
Arguments:
- density: bfloat16 [1024, 512, 512], P(('grp', 'sib')), may hold values from -9 to 9
- kernel: bfloat16 [512, 256], replicated, may hold values from -0.25 to 0.25
- transfer: float32 [4, 256, 256], replicated, may hold values from -1 to 2, as said below
- target_device: int32 [1024, 16], replicated, may hold values from 0 to 127, all different within a row; in each aligned block of 8 rows (0 to 7, 8 to 15, ...) at most 2 rows name the same one
- target_slot: int32 [1024, 16], replicated, may hold values from 0 to 7
- cycle_rows: int32 [1024, 32], replicated, may hold values from 0 to 511, as said below
Outputs:
- leaf_factor: float32 [1024, 256, 256], P(('grp', 'sib'))
- tree_factor: float32 [128, 256, 256], P(('grp', 'sib'))
The draws below stay inside these ranges and needn't reach their ends.
Inputs may be any that keep to these rules, and one draw needn't show every extreme that they name: `target_device`: each row names distinct devices; the 8 rows of one device name each device at most 2 times, and some device exactly 2 times. Each level's transfer matrix is invertible. `cycle_rows`: the cycle of each target cluster lies within one of the four blocks of 128 consecutive longitudes.
All inputs are finite; a program needn't handle non-finite values.
Results may differ from the reference program's by a relative error of at most 0.0024.
Values may be sent and summed in bfloat16 or wider, within the bound.
A program may use at most 64 MiB of HBM per device.

```python
import math
import jax
import jax.numpy as jnp
import numpy as np
from jax import lax

RANK = 256
LC = 512
LONS = 512
LEAF_DEV = 8
NT = 16
CYCLE = 32
LEAVES = 1024
CAP = 2
N_GRP = 8
N_SIB = 16
DEVICES = 128


def draw_transfer(key, part):
    noise = jnp.clip(jax.random.normal(key, (4, RANK, RANK), jnp.float32), -4.0, 4.0)
    rows_iota = lax.broadcasted_iota(jnp.int32, (RANK, RANK), 0)
    cols_iota = lax.broadcasted_iota(jnp.int32, (RANK, RANK), 1)
    identity = (rows_iota == cols_iota).astype(jnp.float32)
    return identity[None] + 0.3 / math.sqrt(RANK) * noise


def draw_density(key, part):
    noise_key = jax.random.fold_in(key, 11)
    sector_key = jax.random.fold_in(key, 23)
    noise = jnp.clip(jax.random.normal(noise_key, (LEAVES, LONS, LC), jnp.float32), -6.0, 6.0)
    sector_means = jnp.clip(jax.random.normal(sector_key, (4, LC), jnp.float32), -4.0, 4.0)
    lon_sector = jnp.arange(LONS, dtype=jnp.int32) // (LONS // 4)
    shifted = 0.7 * sector_means[lon_sector]
    return (noise + shifted[None]).astype(jnp.bfloat16)


def draw_cycle_rows(key, part):
    width = LONS // 4
    leaf_iota = jnp.arange(LEAVES, dtype=jnp.int32)
    position = leaf_iota // LEAF_DEV % 32
    mixed = jnp.bitwise_xor(jnp.bitwise_xor(position, position // 4), position // 16)
    sector = jnp.bitwise_and(mixed, 3)
    offsets = jax.random.randint(jax.random.fold_in(key, 37), (LEAVES, CYCLE), 0, width, dtype=jnp.int32)
    return (sector[:, None] * width + offsets).astype(jnp.int32)


def plant(result, own_key, low, largest):
    longest = result.shape.index(max(result.shape))
    spots = []
    for shift in (0, 1):
        where = [jax.random.randint(jax.random.fold_in(own_key, axis), (), 0, length) for axis, length in enumerate(result.shape)]
        where[longest] = (where[longest] + shift) % result.shape[longest]
        spots.append(tuple(where))
    return result.at[spots[0]].set(low).at[spots[1]].set(largest)


def shared_out(stream_key, own, number, rows, count, top, bound, lean):
    sequence = jax.random.permutation(stream_key, count)
    heavy_load, usual = portions_of(count, rows * top, bound, lean, True), portions_of(count, rows * top, bound, lean, False)
    places = jnp.arange(count)

    def named(lengths, rotation):
        used = int((lengths > 0).sum())
        fixed = max(1, used // 4)
        moved = fixed + (places - fixed + rotation * (used - fixed)) % max(1, count - fixed)
        return jnp.zeros((count,), jnp.int32).at[sequence[jnp.where(places < fixed, places, moved)]].set(jnp.asarray(lengths, jnp.int32))

    lengths = jnp.where(number % 4 == 0, named(heavy_load, number // 4), named(usual, number - number // 4 - 1))
    mixed = jax.random.permutation(jax.random.fold_in(own, 3), count)
    source_of, sink = mixed[0:count // 2 * 2:2], mixed[1:count // 2 * 2:2]
    room = jnp.minimum(lengths[source_of] - 1, bound - lengths[sink]) // 2
    room = jnp.where((source_of == sequence[0]) | (sink == sequence[0]) | (lengths[sink] == 0), 0, jnp.maximum(room, 0))
    moved = jax.random.randint(jax.random.fold_in(own, 4), (count // 2,), 0, 1 << 20) % (room + 1)
    lengths = lengths.at[source_of].add(-moved).at[sink].add(moved)
    members = jnp.searchsorted(jnp.cumsum(lengths), jnp.arange(rows * top), side="right").astype(jnp.int32)
    grid = members.reshape(top, rows).T
    grid = grid[jax.random.permutation(jax.random.fold_in(own, 1), rows)]
    rotation = jax.random.randint(jax.random.fold_in(own, 2), (rows, 1), 0, top)
    return jnp.take_along_axis(grid, (jnp.arange(top)[None, :] + rotation) % top, axis=1)


def portions_of(amount, total, bound, lean, full):
    loads = [(1 << 20) // math.isqrt(standing ** lean) + 1 for standing in range(1, amount + 1)]
    largest = bound if full else min(bound, max(-(-total // amount), total * loads[0] // sum(loads)))
    least = 1 if total - largest >= amount - 1 else 0
    counts, rest = [largest] + [least] * (amount - 1), total - largest - least * (amount - 1)
    while rest > 0:
        free = [i for i in range(1, amount) if counts[i] < largest] or [i for i in range(1, amount) if counts[i] < bound]
        mass, budget = sum([loads[i] for i in free]), rest
        for i in free:
            more = min(bound - counts[i], max(1, budget * loads[i] // mass), rest)
            counts[i] = counts[i] + more
            rest = rest - more
    return np.array(counts)


def bell_draw(rng, shape, scale, reach, kind=jnp.bfloat16):
    array = jax.random.normal(rng, shape, jnp.float32) * scale
    return jnp.minimum(jnp.maximum(array, -reach), reach).astype(kind)


def setup_inputs(seed: int = 0) -> dict:
    seeds = jax.random.split(jax.random.key(seed), 7)
    density = draw_density(jax.random.fold_in(seeds[6], 71), 0)
    kernel = bell_draw(seeds[1], (LC, RANK), LC ** -0.5, 0.25)
    transfer = draw_transfer(jax.random.fold_in(seeds[6], 71), 0)
    target_device_keys = jax.random.split(jax.random.fold_in(seeds[3], 1), LEAVES // LEAF_DEV)
    target_device_turns = jax.random.permutation(jax.random.fold_in(seeds[3], 3), LEAVES // LEAF_DEV)
    target_device = jax.vmap(lambda own, number: shared_out(jax.random.fold_in(seeds[3], 2), own, number, LEAF_DEV, DEVICES, NT, CAP, 2))(target_device_keys, target_device_turns).reshape((LEAVES, NT))
    target_slot = plant(jax.random.randint(seeds[4], (LEAVES, NT), 0, LEAF_DEV), jax.random.fold_in(seeds[4], 1), 0, LEAF_DEV - 1).astype(jnp.int32)
    cycle_rows = draw_cycle_rows(jax.random.fold_in(seeds[6], 71), 0)
    return dict(density=density, kernel=kernel, transfer=transfer, target_device=target_device, target_slot=target_slot, cycle_rows=cycle_rows)


def congruent(matrix, factor):
    inner = jnp.matmul(factor.T, matrix, precision=lax.Precision.HIGHEST)
    return jnp.matmul(inner, factor, precision=lax.Precision.HIGHEST)

def reference(density, kernel, transfer, target_device, target_slot, cycle_rows):
    correlated = lax.map(lambda single: jnp.dot(single.astype(jnp.float32), kernel.astype(jnp.float32), preferred_element_type=jnp.float32).astype(jnp.bfloat16), density)
    targets = (target_device * LEAF_DEV + target_slot).astype(jnp.int32)

    def add_source(running, element):
        source_rows, source_targets = element
        picked = source_rows[cycle_rows[source_targets]].astype(jnp.float32)
        terms = jnp.einsum('nrk,nrl->nkl', picked, picked, precision=lax.Precision.HIGHEST)
        return (running.at[source_targets].add(terms), None)
    running, _ = lax.scan(add_source, jnp.zeros((LEAVES, RANK, RANK), jnp.float32), (correlated, targets))
    identity = jnp.eye(RANK, dtype=jnp.float32)
    gram = identity[None] + running / CYCLE
    leaf_factor = jnp.linalg.cholesky(gram)
    level = gram
    for level_index in range(4):
        traces = jnp.trace(level, axis1=1, axis2=2)
        scaled = RANK * level / traces[:, None, None]
        summed = scaled.reshape(-1, 4, RANK, RANK).sum(axis=1)
        level = congruent(summed, transfer[level_index])
    roots = jnp.linalg.cholesky(level)
    chosen = jnp.arange(N_GRP * N_SIB, dtype=jnp.int32) * LEAF_DEV // 256
    return (leaf_factor, roots[chosen])
```

```python
import functools

import jax
import jax.numpy as jnp
from jax import lax
from jax.experimental import pallas as pl
from jax.experimental.pallas import tpu as pltpu
from jax.sharding import PartitionSpec as P

F32 = jnp.float32
BF16 = jnp.bfloat16
I32 = jnp.int32
MESH = pl.DeviceIdType.MESH
VMEM = pl.BlockSpec(memory_space=pltpu.VMEM)

RANK = 256
LEAF_DEV = 8
CYCLE = 32
N_SIB = 16
DEVICES = 128
TREE = 32


def iota(shape, dim):
    return lax.broadcasted_iota(I32, shape, dim)


def exact_dot(a, b, dims):
    return lax.dot_general(
        a.astype(BF16), b.astype(BF16), (dims, ((), ())), preferred_element_type=F32
    )


def full_dot(a, b, dims):
    return lax.dot_general(
        a, b, (dims, ((), ())), preferred_element_type=F32, precision=lax.Precision.HIGHEST
    )


def own_device():
    return lax.axis_index("grp") * N_SIB + lax.axis_index("sib")


def chain_kernel(t_ref, q_ref, p_ref):
    def scaled(x):
        return x / jnp.max(jnp.abs(x))

    chain = scaled(t_ref[0])
    for level in range(3):
        q_ref[level] = full_dot(chain, chain, ((1,), (1,)))
        chain = full_dot(chain, t_ref[level + 1], ((1,), (0,)))
        if level < 2:
            chain = scaled(chain)
    p_ref[...] = chain


def pack_kernel(dens, kern, tgt, cyc, out, picks, slot_v, slot_s, hot, samples, sem):
    source = pl.program_id(0)
    n_list = 16

    @pl.when(source == 0)
    def _():
        out[...] = jnp.zeros_like(out)
        own = tgt[pl.ds(own_device(), 1), :]
        dest = own // LEAF_DEV
        hits = (iota((DEVICES, 128), 0) == dest).astype(F32)
        upper = (iota((128, 128), 0) < iota((128, 128), 1)).astype(F32)
        before = exact_dot(hits, upper, ((1,), (0,)))
        ahead = jnp.sum(before * hits, axis=0, keepdims=True)
        slot = dest * 2 + ahead.astype(I32)
        slot_v[...] = jnp.broadcast_to(slot, slot_v.shape)
        copy = pltpu.make_async_copy(slot_v, slot_s, sem)
        copy.start()
        which = (iota((1024, 128), 0) == own).astype(F32)
        rows = cyc[...]
        high = exact_dot((rows // 128).astype(F32), which, ((0,), (0,)))
        low = exact_dot((rows % 128).astype(F32), which, ((0,), (0,)))
        picks[...] = high * 128.0 + low
        copy.wait()

    corr = jnp.dot(dens[0], kern[...], preferred_element_type=F32).astype(BF16)
    mine = pltpu.roll(picks[...], lax.rem(128 - n_list * source, 128), 1)
    lon = iota((CYCLE, 512), 1).astype(F32)
    for k in range(n_list):
        hot[CYCLE * k : CYCLE * (k + 1), :] = (
            jnp.broadcast_to(mine[:, k : k + 1], (CYCLE, 512)) == lon
        ).astype(BF16)
    samples[...] = jnp.dot(hot[...], corr, preferred_element_type=F32).astype(BF16)
    for k in range(n_list):
        out[slot_s[0, source * n_list + k]] = samples[CYCLE * k : CYCLE * (k + 1), :]


ORDER = 384


def gram_kernel(arrived, tgt, q_ref, gram, aug, table_v, table_s, chunk, sem):
    me = own_device()
    targets = tgt[...]
    match = (targets // LEAF_DEV == me).astype(F32)
    leaf = (targets % LEAF_DEV).astype(F32) + 1.0
    upper = (iota((128, 128), 0) < iota((128, 128), 1)).astype(F32)
    before = exact_dot(match, upper, ((1,), (0,)))
    ones = jnp.ones((LEAF_DEV, 128), F32)
    named = match * leaf
    first = exact_dot(ones, jnp.where(before < 0.5, named, 0.0), ((1,), (1,)))
    second = exact_dot(ones, jnp.where(before > 0.5, named, 0.0), ((1,), (1,)))
    slot_leaf = jnp.concatenate([first, second], axis=1)
    lane = iota((LEAF_DEV, 256), 1)
    held = (slot_leaf == (iota((LEAF_DEV, 256), 0) + 1).astype(F32)).astype(F32)
    upper2 = (iota((256, 256), 0) < iota((256, 256), 1)).astype(F32)
    rank = exact_dot(held, upper2, ((1,), (0,)))
    count = jnp.sum(held, axis=1, keepdims=True)
    chunks = (count.astype(I32) + 7) // 8
    wide = jnp.broadcast_to(chunks, (LEAF_DEV, 128)).astype(F32)
    lower = (iota((LEAF_DEV, LEAF_DEV), 1) < iota((LEAF_DEV, LEAF_DEV), 0)).astype(F32)
    start = exact_dot(lower, wide, ((1,), (0,)))
    start2 = jnp.concatenate([start, start], axis=1) * 8.0
    place = jnp.sum(held * (start2 + rank + 1.0), axis=0, keepdims=True) - 1.0
    onto = (iota((ORDER, 256), 0).astype(F32) == place).astype(F32)
    value = (2 * (lane % 128) + lane // 128 + 1).astype(F32)
    order = exact_dot(value, onto, ((1,), (1,))).astype(I32) - 1
    table_v[0:8, :] = order
    table_v[8:16, 0:128] = jnp.broadcast_to(chunks, (LEAF_DEV, 128))
    table_v[16:24, 0:128] = start.astype(I32)
    copy = pltpu.make_async_copy(table_v, table_s, sem)
    copy.start()
    gram[...] = jnp.zeros_like(gram)
    copy.wait()

    most = table_s[8, 0]
    for j in range(1, LEAF_DEV):
        most = jnp.maximum(most, table_s[8 + j, 0])

    def add_chunk(c, carry):
        for j in range(LEAF_DEV):
            inside = c < table_s[8 + j, 0]
            base = jnp.where(inside, (table_s[16 + j, 0] + c) * 8, 0)
            for b in range(8):
                index = table_s[0, base + b]
                live = jnp.logical_and(inside, index >= 0)
                block = arrived[jnp.maximum(index, 0)]
                chunk[j, CYCLE * b : CYCLE * (b + 1), :] = jnp.where(
                    live, block, jnp.zeros_like(block)
                )
        for j in range(LEAF_DEV):
            rows = chunk[j]
            gram[j] = gram[j] + lax.dot_general(
                rows, rows, (((0,), (0,)), ((), ())), preferred_element_type=F32
            )
        return carry

    lax.fori_loop(0, most, add_chunk, 0)

    row = iota((RANK, RANK), 0)
    col = iota((RANK, RANK), 1)
    eye = (row == col).astype(F32)

    def total(x):
        return jnp.sum(jnp.sum(x, axis=0, keepdims=True), axis=1, keepdims=True)

    whole = None
    for node in range(2):
        merged = None
        for child in range(4):
            j = 4 * node + child
            one = gram[j] * (1.0 / CYCLE) + eye
            gram[j] = one
            scaled = one * (RANK / total(one * eye))
            merged = scaled if merged is None else merged + scaled
        scaled = merged * (RANK / total(merged * q_ref[0]))
        whole = scaled if whole is None else whole + scaled
    aug[:, 0:RANK] = whole
    second_trace = total(whole * q_ref[1])
    third_trace = total(whole * q_ref[2])
    aug[:, RANK : RANK + 128] = jnp.where(
        iota((RANK, 128), 0) % 2 == 0, second_trace, third_trace
    )


def tree_kernel(aug, p_ref, root, first, second, part, send_a, recv_a, send_b, recv_b, local):
    grp = lax.axis_index("grp")
    sib = lax.axis_index("sib")
    base = (grp // 2) * 2
    me = (grp % 2) * N_SIB + sib

    def device(index):
        return (base + index // N_SIB, index % N_SIB)

    barrier = pltpu.get_barrier_semaphore()

    def greet(k, carry):
        pl.semaphore_signal(
            barrier, inc=1, device_id=device((me + k) % TREE), device_id_type=MESH
        )
        return carry

    lax.fori_loop(1, TREE, greet, 0)
    pl.semaphore_wait(barrier, TREE - 1)

    def rows_copy(k, target, source):
        return pltpu.make_async_remote_copy(
            src_ref=aug.at[pl.ds(pl.multiple_of(target * 8, 8), 8), :],
            dst_ref=first.at[source],
            send_sem=send_a.at[k],
            recv_sem=recv_a.at[k],
            device_id=device(target),
            device_id_type=MESH,
        )

    def part_copy(k, target, source):
        return pltpu.make_async_remote_copy(
            src_ref=part,
            dst_ref=second.at[pl.ds(pl.multiple_of(source * 8, 8), 8), :],
            send_sem=send_b.at[k],
            recv_sem=recv_b.at[k],
            device_id=device(target),
            device_id_type=MESH,
        )

    def run(make):
        def start(k, carry):
            make(k, (me + k) % TREE, me).start()
            return carry

        lax.fori_loop(1, TREE, start, 0)

    def wait(make):
        def arrive(k, carry):
            make(k, (me + k) % TREE, (me - k + TREE) % TREE).wait_recv()
            return carry

        lax.fori_loop(1, TREE, arrive, 0)

    def drain(make):
        def sent(k, carry):
            make(k, (me + k) % TREE, me).wait_send()
            return carry

        lax.fori_loop(1, TREE, sent, 0)

    run(rows_copy)
    first[me] = aug[pl.ds(pl.multiple_of(me * 8, 8), 8), :]
    wait(rows_copy)

    gathered = None
    for quad in range(4):
        merged = None
        trace = None
        for pair in range(4):
            d = quad * 8 + pair * 2
            both = first[d] + first[d + 1]
            weight = RANK / both[0:1, RANK : RANK + 128]
            third = both[1:2, RANK : RANK + 128] * weight
            weight2 = jnp.concatenate([weight, weight], axis=1)
            scaled = both[:, 0:RANK] * weight2
            merged = scaled if merged is None else merged + scaled
            trace = third if trace is None else trace + third
        weight = RANK / trace
        scaled = merged * jnp.concatenate([weight, weight], axis=1)
        gathered = scaled if gathered is None else gathered + scaled
    part[...] = full_dot(gathered, p_ref[...], ((1,), (0,)))
    run(part_copy)
    second[pl.ds(pl.multiple_of(me * 8, 8), 8), :] = part[...]
    wait(part_copy)
    root[...] = full_dot(p_ref[...], second[...], ((0,), (0,)))
    drain(rows_copy)
    drain(part_copy)


BLOCK = 64


def factor_block(rows):
    n = rows[0].shape[0]
    sub = iota((n, 8, 128), 1)
    for r in range(len(rows)):
        scale = None
        for c in range(8):
            i = 8 * r + c
            cols = [jnp.broadcast_to(x[:, :, i : i + 1], (n, 8, 128)) for x in rows[r:]]
            s = lax.rsqrt(cols[0][:, c : c + 1, :])
            pivot = rows[r][:, c : c + 1, :] * (s * s)
            wide = jnp.broadcast_to(s, (n, 8, 128))
            scale = wide if scale is None else jnp.where(sub >= c, wide, scale)
            if c < 7:
                rows[r] = rows[r] - jnp.where(sub > c, cols[0], 0.0) * pivot
            for q in range(r + 1, len(rows)):
                rows[q] = rows[q] - cols[q - r] * pivot
        rows[r] = rows[r] * scale
    return rows


def cholesky_kernel(gram, root, leaf_out, root_out, work):
    n = LEAF_DEV + 1
    work[0:LEAF_DEV] = gram[...]
    work[LEAF_DEV] = root[...]
    lane = iota((BLOCK, 128), 1)
    eye = (lane - BLOCK == iota((BLOCK, 128), 0)).astype(F32)
    for step in range(RANK // BLOCK):
        r0 = BLOCK * step
        base = 128 * (step // 2)
        odd = step % 2
        block = work[:, r0 : r0 + BLOCK, base : base + 128]
        if odd:
            block = pltpu.roll(block, BLOCK, 2)
        block = jnp.where((lane < BLOCK)[None], block, eye[None])
        rows = factor_block([block[:, 8 * q : 8 * q + 8, :] for q in range(BLOCK // 8)])
        inverse = jnp.concatenate(rows, axis=1)
        if not odd:
            inverse = pltpu.roll(inverse, BLOCK, 2)
        inverse = jnp.where(((lane >= BLOCK) if odd else (lane < BLOCK))[None], inverse, 0.0)
        height = RANK - r0
        below = iota((height, BLOCK), 0) >= iota((height, BLOCK), 1)
        for m in range(n):
            panel = full_dot(work[m, r0:, base : base + 128], inverse[m], ((1,), (1,)))
            panel = jnp.where(below, panel, 0.0)
            out = leaf_out.at[m] if m < LEAF_DEV else root_out.at[0]
            if r0:
                out[0:r0, r0 : r0 + BLOCK] = jnp.zeros((r0, BLOCK), F32)
            out[r0:, r0 : r0 + BLOCK] = panel
            if height > BLOCK:
                c0 = 128 * ((step + 1) // 2)
                if c0 >= r0:
                    cols = panel[c0 - r0 :]
                else:
                    cols = jnp.concatenate([jnp.zeros((r0 - c0, BLOCK), F32), panel], axis=0)
                work[m, r0 + BLOCK :, c0:] = work[m, r0 + BLOCK :, c0:] - full_dot(
                    panel[BLOCK:], cols, ((1,), (1,))
                )


def sds(shape, dtype):
    return jax.ShapeDtypeStruct(shape, dtype)


def local(density, kernel, transfer, target_device, target_slot, cycle_rows):
    params = functools.partial(pltpu.CompilerParams, vmem_limit_bytes=48 * 2**20)
    targets = (target_device * LEAF_DEV + target_slot).reshape(DEVICES, 128)
    packed = pl.pallas_call(
        pack_kernel,
        grid=(LEAF_DEV,),
        out_shape=sds((2 * DEVICES, CYCLE, RANK), BF16),
        in_specs=[
            pl.BlockSpec((1, 512, 512), lambda s: (s, 0, 0)),
            pl.BlockSpec((512, RANK), lambda s: (0, 0)),
            pl.BlockSpec((DEVICES, 128), lambda s: (0, 0)),
            pl.BlockSpec((1024, CYCLE), lambda s: (0, 0)),
        ],
        out_specs=pl.BlockSpec((2 * DEVICES, CYCLE, RANK), lambda s: (0, 0, 0)),
        scratch_shapes=[
            pltpu.VMEM((CYCLE, 128), F32),
            pltpu.VMEM((8, 128), I32),
            pltpu.SMEM((8, 128), I32),
            pltpu.VMEM((512, 512), BF16),
            pltpu.VMEM((512, RANK), BF16),
            pltpu.SemaphoreType.DMA,
        ],
        compiler_params=params(),
        name="pack",
    )(density, kernel, targets, cycle_rows)
    arrived = lax.all_to_all(
        packed.reshape(DEVICES, 2, CYCLE, RANK),
        ("grp", "sib"),
        split_axis=0,
        concat_axis=0,
        tiled=True,
    ).reshape(2 * DEVICES, CYCLE, RANK)
    squares, chain = pl.pallas_call(
        chain_kernel,
        out_shape=(sds((3, RANK, RANK), F32), sds((RANK, RANK), F32)),
        in_specs=[VMEM],
        out_specs=(VMEM, VMEM),
        compiler_params=params(),
        cost_estimate=pl.CostEstimate(
            flops=6 * 6 * 2 * RANK**3, bytes_accessed=8 * 4 * RANK**2, transcendentals=0
        ),
        name="chain",
    )(transfer)
    gram, augmented = pl.pallas_call(
        gram_kernel,
        out_shape=(sds((LEAF_DEV, RANK, RANK), F32), sds((RANK, RANK + 128), F32)),
        in_specs=[VMEM] * 3,
        out_specs=(VMEM, VMEM),
        scratch_shapes=[
            pltpu.VMEM((24, ORDER), I32),
            pltpu.SMEM((24, ORDER), I32),
            pltpu.VMEM((LEAF_DEV, 256, RANK), BF16),
            pltpu.SemaphoreType.DMA,
        ],
        compiler_params=params(),
        name="gram",
    )(arrived, targets, squares)
    root = pl.pallas_call(
        tree_kernel,
        out_shape=sds((RANK, RANK), F32),
        in_specs=[VMEM] * 2,
        out_specs=VMEM,
        scratch_shapes=[
            pltpu.VMEM((TREE, 8, RANK + 128), F32),
            pltpu.VMEM((RANK, RANK), F32),
            pltpu.VMEM((8, RANK), F32),
            pltpu.SemaphoreType.DMA((TREE,)),
            pltpu.SemaphoreType.DMA((TREE,)),
            pltpu.SemaphoreType.DMA((TREE,)),
            pltpu.SemaphoreType.DMA((TREE,)),
            pltpu.SemaphoreType.DMA,
        ],
        compiler_params=params(collective_id=1, has_side_effects=True),
        name="tree",
    )(augmented, chain)
    return pl.pallas_call(
        cholesky_kernel,
        out_shape=(sds((LEAF_DEV, RANK, RANK), F32), sds((1, RANK, RANK), F32)),
        in_specs=[VMEM] * 2,
        out_specs=(VMEM, VMEM),
        scratch_shapes=[pltpu.VMEM((LEAF_DEV + 1, RANK, RANK), F32)],
        compiler_params=params(),
        name="cholesky",
    )(gram, root)


def solution(mesh):
    return jax.shard_map(
        local,
        mesh=mesh,
        in_specs=(P(("grp", "sib"), None, None), P(), P(), P(), P(), P()),
        out_specs=(P(("grp", "sib"), None, None), P(("grp", "sib"), None, None)),
        check_vma=False,
    )
```

```python
import functools

import jax
import jax.numpy as jnp
from jax import lax
from jax.experimental import pallas as pl
from jax.experimental.pallas import tpu as pltpu
from jax.sharding import PartitionSpec as P

F32 = jnp.float32
BF16 = jnp.bfloat16
I32 = jnp.int32
MESH = pl.DeviceIdType.MESH
VMEM = pl.BlockSpec(memory_space=pltpu.VMEM)

RANK = 256
LEAF_DEV = 8
CYCLE = 32
N_SIB = 16
DEVICES = 128
TREE = 32


def iota(shape, dim):
    return lax.broadcasted_iota(I32, shape, dim)


def exact_dot(a, b, dims):
    return lax.dot_general(
        a.astype(BF16), b.astype(BF16), (dims, ((), ())), preferred_element_type=F32
    )


def full_dot(a, b, dims):
    return lax.dot_general(
        a, b, (dims, ((), ())), preferred_element_type=F32, precision=lax.Precision.HIGHEST
    )


def own_device():
    return lax.axis_index("grp") * N_SIB + lax.axis_index("sib")


def pack_kernel(dens, kern, tgt, cyc, out, owners, picks, slot_v, slot_s, hot, samples, sem):
    source = pl.program_id(0)
    n_list = 16

    @pl.when(source == 0)
    def _():
        out[...] = jnp.zeros_like(out)
        own = tgt[pl.ds(own_device(), 1), :]
        dest = own // LEAF_DEV
        hits = (iota((DEVICES, 128), 0) == dest).astype(F32)
        upper = (iota((128, 128), 0) < iota((128, 128), 1)).astype(F32)
        before = exact_dot(hits, upper, ((1,), (0,)))
        ahead = jnp.sum(before * hits, axis=0, keepdims=True)
        slot = dest * 2 + ahead.astype(I32)
        slot_v[...] = jnp.broadcast_to(slot, slot_v.shape)
        copy = pltpu.make_async_copy(slot_v, slot_s, sem)
        copy.start()
        which = (iota((1024, 128), 0) == own).astype(F32)
        rows = cyc[...]
        high = exact_dot((rows // 128).astype(F32), which, ((0,), (0,)))
        low = exact_dot((rows % 128).astype(F32), which, ((0,), (0,)))
        picks[...] = high * 128.0 + low
        targets = tgt[...]
        match = (targets // LEAF_DEV == own_device()).astype(F32)
        earlier = exact_dot(match, upper, ((1,), (0,)))
        named = match * ((targets % LEAF_DEV).astype(F32) + 1.0)
        first = jnp.sum(jnp.where(earlier < 0.5, named, 0.0), axis=1, keepdims=True)
        second = jnp.sum(jnp.where(earlier > 0.5, named, 0.0), axis=1, keepdims=True)
        owners[...] = jnp.where(iota((DEVICES, 128), 1) % 64 < CYCLE, first, second)
        copy.wait()

    corr = jnp.dot(dens[0], kern[...], preferred_element_type=F32).astype(BF16)
    mine = pltpu.roll(picks[...], lax.rem(128 - n_list * source, 128), 1)
    lon = iota((CYCLE, 512), 1).astype(F32)
    for k in range(n_list):
        hot[CYCLE * k : CYCLE * (k + 1), :] = (
            jnp.broadcast_to(mine[:, k : k + 1], (CYCLE, 512)) == lon
        ).astype(BF16)
    samples[...] = jnp.dot(hot[...], corr, preferred_element_type=F32).astype(BF16)
    for k in range(n_list):
        out[slot_s[0, source * n_list + k]] = samples[CYCLE * k : CYCLE * (k + 1), :]


ROUNDS = 16
PER_ROUND = 8


def exchange_kernel(
    packed, owners, t_ref, gram, root,
    arrived, sums, q_ref, p_ref, aug, first, second, part,
    send_x, recv_x, send_a, recv_a, send_b, recv_b, local,
):
    grp = lax.axis_index("grp")
    sib = lax.axis_index("sib")
    my_x, my_c = grp // 2, grp % 2
    my_y, my_z = sib // 4, sib % 4

    def place(it, lane, sign):
        dz, dc = lane // 2, lane % 2
        dy = (it + dz) % 4
        dx = (it // 4 + dy) % 4
        x = (my_x + sign * dx + 4) % 4
        y = (my_y + sign * dy + 4) % 4
        z = (my_z + sign * dz + 4) % 4
        return x * 2 + (my_c + dc) % 2, y * 4 + z

    def each(it, act):
        @pl.when(it > 0)
        def _():
            act(it, 0)

        for lane in range(1, PER_ROUND):
            act(it, lane)

    def rounds(act):
        def body(it, carry):
            each(it, act)
            return carry

        lax.fori_loop(0, ROUNDS, body, 0)

    barrier = pltpu.get_barrier_semaphore()

    def greet(it, lane):
        pl.semaphore_signal(barrier, inc=1, device_id=place(it, lane, 1), device_id_type=MESH)

    rounds(greet)
    pl.semaphore_wait(barrier, DEVICES - 1)

    def block_copy(it, lane):
        to = place(it, lane, 1)
        k = it * PER_ROUND + lane
        return pltpu.make_async_remote_copy(
            src_ref=packed.at[to[0] * N_SIB + to[1]],
            dst_ref=arrived.at[k],
            send_sem=send_x.at[k],
            recv_sem=recv_x.at[k],
            device_id=to,
            device_id_type=MESH,
        )

    rounds(lambda it, lane: block_copy(it, lane).start())
    own = pltpu.make_async_copy(packed.at[grp * N_SIB + sib], arrived.at[0], local)
    own.start()

    def scaled(x):
        return x / jnp.max(jnp.abs(x))

    chain = scaled(t_ref[0])
    for level in range(3):
        q_ref[level] = full_dot(chain, chain, ((1,), (1,)))
        chain = full_dot(chain, t_ref[level + 1], ((1,), (0,)))
        if level < 2:
            chain = scaled(chain)
    p_ref[...] = chain
    sums[...] = jnp.zeros_like(sums)
    own.wait()

    def leaves(it, lane):
        source = place(it, lane, -1)
        return owners[pl.ds(source[0] * N_SIB + source[1], 1), :]

    def add_round(it, carry):
        each(it, lambda i, lane: block_copy(i, lane).wait_recv())
        low = iota((1, 128), 1) < 64
        for half in range(2):
            start = pl.multiple_of(it * PER_ROUND, PER_ROUND) + 4 * half
            rows = arrived[pl.ds(start, 4)].reshape(4 * 2 * CYCLE, RANK)
            leaf = jnp.concatenate(
                [
                    jnp.where(low, leaves(it, 4 * half + b), leaves(it, 4 * half + b + 1))
                    for b in (0, 2)
                ],
                axis=1,
            )
            turned = rows.T
            for j in range(LEAF_DEV):
                mask = (leaf == float(j + 1)).astype(BF16)
                sums[j] = sums[j] + jnp.dot(turned * mask, rows, preferred_element_type=F32)
        return carry

    lax.fori_loop(0, ROUNDS, add_round, 0)

    eye = (iota((RANK, RANK), 0) == iota((RANK, RANK), 1)).astype(F32)

    def total(x):
        return jnp.sum(jnp.sum(x, axis=0, keepdims=True), axis=1, keepdims=True)

    whole = None
    for node in range(2):
        merged = None
        for child in range(4):
            j = 4 * node + child
            one = sums[j] * (1.0 / CYCLE) + eye
            gram[j] = one
            weighted = one * (RANK / total(one * eye))
            merged = weighted if merged is None else merged + weighted
        weighted = merged * (RANK / total(merged * q_ref[0]))
        whole = weighted if whole is None else whole + weighted
    aug[:, 0:RANK] = whole
    second_trace = total(whole * q_ref[1])
    third_trace = total(whole * q_ref[2])
    aug[:, RANK : RANK + 128] = jnp.where(
        iota((RANK, 128), 0) % 2 == 0, second_trace, third_trace
    )

    base = (grp // 2) * 2
    me = (grp % 2) * N_SIB + sib

    def device(index):
        return (base + index // N_SIB, index % N_SIB)

    def rows_copy(k, target, source):
        return pltpu.make_async_remote_copy(
            src_ref=aug.at[pl.ds(pl.multiple_of(target * 8, 8), 8), :],
            dst_ref=first.at[source],
            send_sem=send_a.at[k],
            recv_sem=recv_a.at[k],
            device_id=device(target),
            device_id_type=MESH,
        )

    def part_copy(k, target, source):
        return pltpu.make_async_remote_copy(
            src_ref=part,
            dst_ref=second.at[pl.ds(pl.multiple_of(source * 8, 8), 8), :],
            send_sem=send_b.at[k],
            recv_sem=recv_b.at[k],
            device_id=device(target),
            device_id_type=MESH,
        )

    def run(make):
        def start(k, carry):
            make(k, (me + k) % TREE, me).start()
            return carry

        lax.fori_loop(1, TREE, start, 0)

    def wait(make):
        def arrive(k, carry):
            make(k, (me + k) % TREE, (me - k + TREE) % TREE).wait_recv()
            return carry

        lax.fori_loop(1, TREE, arrive, 0)

    def drain(make):
        def sent(k, carry):
            make(k, (me + k) % TREE, me).wait_send()
            return carry

        lax.fori_loop(1, TREE, sent, 0)

    run(rows_copy)
    first[me] = aug[pl.ds(pl.multiple_of(me * 8, 8), 8), :]
    wait(rows_copy)

    gathered = None
    for quad in range(4):
        merged = None
        trace = None
        for pair in range(4):
            d = quad * 8 + pair * 2
            both = first[d] + first[d + 1]
            weight = RANK / both[0:1, RANK : RANK + 128]
            third = both[1:2, RANK : RANK + 128] * weight
            weight2 = jnp.concatenate([weight, weight], axis=1)
            scaled = both[:, 0:RANK] * weight2
            merged = scaled if merged is None else merged + scaled
            trace = third if trace is None else trace + third
        weight = RANK / trace
        scaled = merged * jnp.concatenate([weight, weight], axis=1)
        gathered = scaled if gathered is None else gathered + scaled
    part[...] = full_dot(gathered, p_ref[...], ((1,), (0,)))
    run(part_copy)
    second[pl.ds(pl.multiple_of(me * 8, 8), 8), :] = part[...]
    wait(part_copy)
    root[...] = full_dot(p_ref[...], second[...], ((0,), (0,)))
    drain(rows_copy)
    drain(part_copy)
    rounds(lambda it, lane: block_copy(it, lane).wait_send())


BLOCK = 64


def factor_block(rows):
    n = rows[0].shape[0]
    sub = iota((n, 8, 128), 1)
    for r in range(len(rows)):
        scale = None
        for c in range(8):
            i = 8 * r + c
            cols = [jnp.broadcast_to(x[:, :, i : i + 1], (n, 8, 128)) for x in rows[r:]]
            s = lax.rsqrt(cols[0][:, c : c + 1, :])
            pivot = rows[r][:, c : c + 1, :] * (s * s)
            wide = jnp.broadcast_to(s, (n, 8, 128))
            scale = wide if scale is None else jnp.where(sub >= c, wide, scale)
            if c < 7:
                rows[r] = rows[r] - jnp.where(sub > c, cols[0], 0.0) * pivot
            for q in range(r + 1, len(rows)):
                rows[q] = rows[q] - cols[q - r] * pivot
        rows[r] = rows[r] * scale
    return rows


def cholesky_kernel(gram, root, leaf_out, root_out, work):
    n = LEAF_DEV + 1
    work[0:LEAF_DEV] = gram[...]
    work[LEAF_DEV] = root[...]
    lane = iota((BLOCK, 128), 1)
    eye = (lane - BLOCK == iota((BLOCK, 128), 0)).astype(F32)
    for step in range(RANK // BLOCK):
        r0 = BLOCK * step
        base = 128 * (step // 2)
        odd = step % 2
        block = work[:, r0 : r0 + BLOCK, base : base + 128]
        if odd:
            block = pltpu.roll(block, BLOCK, 2)
        block = jnp.where((lane < BLOCK)[None], block, eye[None])
        rows = factor_block([block[:, 8 * q : 8 * q + 8, :] for q in range(BLOCK // 8)])
        inverse = jnp.concatenate(rows, axis=1)
        if not odd:
            inverse = pltpu.roll(inverse, BLOCK, 2)
        inverse = jnp.where(((lane >= BLOCK) if odd else (lane < BLOCK))[None], inverse, 0.0)
        height = RANK - r0
        below = iota((height, BLOCK), 0) >= iota((height, BLOCK), 1)
        for m in range(n):
            panel = full_dot(work[m, r0:, base : base + 128], inverse[m], ((1,), (1,)))
            panel = jnp.where(below, panel, 0.0)
            out = leaf_out.at[m] if m < LEAF_DEV else root_out.at[0]
            if r0:
                out[0:r0, r0 : r0 + BLOCK] = jnp.zeros((r0, BLOCK), F32)
            out[r0:, r0 : r0 + BLOCK] = panel
            if height > BLOCK:
                c0 = 128 * ((step + 1) // 2)
                if c0 >= r0:
                    cols = panel[c0 - r0 :]
                else:
                    cols = jnp.concatenate([jnp.zeros((r0 - c0, BLOCK), F32), panel], axis=0)
                work[m, r0 + BLOCK :, c0:] = work[m, r0 + BLOCK :, c0:] - full_dot(
                    panel[BLOCK:], cols, ((1,), (1,))
                )


def sds(shape, dtype):
    return jax.ShapeDtypeStruct(shape, dtype)


def local(density, kernel, transfer, target_device, target_slot, cycle_rows):
    params = functools.partial(pltpu.CompilerParams, vmem_limit_bytes=48 * 2**20)
    targets = (target_device * LEAF_DEV + target_slot).reshape(DEVICES, 128)
    packed, owners = pl.pallas_call(
        pack_kernel,
        grid=(LEAF_DEV,),
        out_shape=(sds((2 * DEVICES, CYCLE, RANK), BF16), sds((DEVICES, 128), F32)),
        in_specs=[
            pl.BlockSpec((1, 512, 512), lambda s: (s, 0, 0)),
            pl.BlockSpec((512, RANK), lambda s: (0, 0)),
            pl.BlockSpec((DEVICES, 128), lambda s: (0, 0)),
            pl.BlockSpec((1024, CYCLE), lambda s: (0, 0)),
        ],
        out_specs=(
            pl.BlockSpec((2 * DEVICES, CYCLE, RANK), lambda s: (0, 0, 0)),
            pl.BlockSpec((DEVICES, 128), lambda s: (0, 0)),
        ),
        scratch_shapes=[
            pltpu.VMEM((CYCLE, 128), F32),
            pltpu.VMEM((8, 128), I32),
            pltpu.SMEM((8, 128), I32),
            pltpu.VMEM((512, 512), BF16),
            pltpu.VMEM((512, RANK), BF16),
            pltpu.SemaphoreType.DMA,
        ],
        compiler_params=params(),
        name="pack",
    )(density, kernel, targets, cycle_rows)
    gram, root = pl.pallas_call(
        exchange_kernel,
        out_shape=(sds((LEAF_DEV, RANK, RANK), F32), sds((RANK, RANK), F32)),
        in_specs=[pl.BlockSpec(memory_space=pl.ANY), VMEM, VMEM],
        out_specs=(VMEM, VMEM),
        scratch_shapes=[
            pltpu.VMEM((DEVICES, 2, CYCLE, RANK), BF16),
            pltpu.VMEM((LEAF_DEV, RANK, RANK), F32),
            pltpu.VMEM((3, RANK, RANK), F32),
            pltpu.VMEM((RANK, RANK), F32),
            pltpu.VMEM((RANK, RANK + 128), F32),
            pltpu.VMEM((TREE, 8, RANK + 128), F32),
            pltpu.VMEM((RANK, RANK), F32),
            pltpu.VMEM((8, RANK), F32),
            pltpu.SemaphoreType.DMA((DEVICES,)),
            pltpu.SemaphoreType.DMA((DEVICES,)),
            pltpu.SemaphoreType.DMA((TREE,)),
            pltpu.SemaphoreType.DMA((TREE,)),
            pltpu.SemaphoreType.DMA((TREE,)),
            pltpu.SemaphoreType.DMA((TREE,)),
            pltpu.SemaphoreType.DMA,
        ],
        compiler_params=params(collective_id=1, has_side_effects=True),
        name="exchange",
    )(packed.reshape(DEVICES, 2, CYCLE, RANK), owners, transfer)
    return pl.pallas_call(
        cholesky_kernel,
        out_shape=(sds((LEAF_DEV, RANK, RANK), F32), sds((1, RANK, RANK), F32)),
        in_specs=[VMEM] * 2,
        out_specs=(VMEM, VMEM),
        scratch_shapes=[pltpu.VMEM((LEAF_DEV + 1, RANK, RANK), F32)],
        compiler_params=params(),
        name="cholesky",
    )(gram, root)


def solution(mesh):
    return jax.shard_map(
        local,
        mesh=mesh,
        in_specs=(P(("grp", "sib"), None, None), P(), P(), P(), P(), P()),
        out_specs=(P(("grp", "sib"), None, None), P(("grp", "sib"), None, None)),
        check_vma=False,
    )
```

```python
import functools

import jax
import jax.numpy as jnp
from jax import lax
from jax.experimental import pallas as pl
from jax.experimental.pallas import tpu as pltpu
from jax.sharding import PartitionSpec as P

F32 = jnp.float32
BF16 = jnp.bfloat16
I32 = jnp.int32
MESH = pl.DeviceIdType.MESH
VMEM = pl.BlockSpec(memory_space=pltpu.VMEM)

RANK = 256
LEAF_DEV = 8
CYCLE = 32
N_SIB = 16
DEVICES = 128
TREE = 32


def iota(shape, dim):
    return lax.broadcasted_iota(I32, shape, dim)


def exact_dot(a, b, dims):
    return lax.dot_general(
        a.astype(BF16), b.astype(BF16), (dims, ((), ())), preferred_element_type=F32
    )


def full_dot(a, b, dims):
    return lax.dot_general(
        a, b, (dims, ((), ())), preferred_element_type=F32, precision=lax.Precision.HIGHEST
    )


def own_device():
    return lax.axis_index("grp") * N_SIB + lax.axis_index("sib")


def pack_kernel(
    dens, kern, dev, slot, cyc, out, owners,
    picks, slot_v, slot_s, hot, samples, zeros, zero_sem, slot_sem, sem,
):
    source = pl.program_id(0)
    n_list = 16
    fill = zeros.shape[0]

    def clear(part):
        return pltpu.make_async_copy(zeros, out.at[pl.ds(part * fill, fill)], zero_sem.at[part])

    slots_down = pltpu.make_async_copy(slot_v, slot_s, slot_sem)

    @pl.when(source == 0)
    def _():
        zeros[...] = jnp.zeros_like(zeros)
        for part in range(2 * DEVICES // fill):
            clear(part).start()
        me = own_device()
        lane = iota((1024, 128), 1)
        row = iota((1024, 128), 0)
        mine = (row == me * LEAF_DEV + lane % LEAF_DEV).astype(F32)
        diagonal = iota((n_list, 128), 0) == iota((n_list, 128), 1) // LEAF_DEV

        def own_entries(x):
            wide = exact_dot(x.astype(F32), mine, ((1,), (0,)))
            return jnp.sum(jnp.where(diagonal, wide, 0.0), axis=0, keepdims=True).astype(I32)

        dest, leaf = own_entries(dev[...]), own_entries(slot[...])
        hits = (iota((DEVICES, 128), 0) == dest).astype(F32)
        earlier = (iota((128, 128), 0) % LEAF_DEV < iota((128, 128), 1) % LEAF_DEV).astype(F32)
        ahead = jnp.sum(exact_dot(hits, earlier, ((1,), (0,))) * hits, axis=0, keepdims=True)
        slot_v[...] = jnp.broadcast_to(dest * 2 + ahead.astype(I32), slot_v.shape)
        slots_down.start()
        which = (row == dest * LEAF_DEV + leaf).astype(F32)
        rows = cyc[...]
        high = exact_dot((rows // 128).astype(F32), which, ((1,), (0,)))
        low = exact_dot((rows % 128).astype(F32), which, ((1,), (0,)))
        picks[...] = high * 128.0 + low
        match = dev[...] == me
        named = jnp.sum(jnp.where(match, slot[...] + 1, 0), axis=0, keepdims=True).astype(F32)
        named = jnp.concatenate(
            [named[:, 128 * i : 128 * (i + 1)] for i in range(LEAF_DEV)], axis=0
        )
        block = jnp.logical_and(
            iota((128, 128), 0) // LEAF_DEV == iota((128, 128), 1) // LEAF_DEV,
            iota((128, 128), 0) < iota((128, 128), 1),
        )
        before = exact_dot((named > 0.5).astype(F32), block.astype(F32), ((1,), (0,)))
        here = iota((DEVICES, 128), 1) // LEAF_DEV == iota((DEVICES, 128), 0) % n_list

        def per_device(x):
            wide = jnp.broadcast_to(x[:, None, :], (LEAF_DEV, n_list, 128)).reshape(DEVICES, 128)
            return jnp.sum(jnp.where(here, wide, 0.0), axis=1, keepdims=True)

        first = per_device(jnp.where(before < 0.5, named, 0.0))
        second = per_device(jnp.where(before > 0.5, named, 0.0))
        owners[...] = jnp.where(iota((DEVICES, 128), 1) % 64 < CYCLE, first, second)

    corr = jnp.dot(dens[0], kern[...], preferred_element_type=F32).astype(BF16)
    turned = pltpu.roll(picks[...], lax.rem(128 - source, 128), 1)
    lon = iota((CYCLE, 512), 1).astype(F32)
    for k in range(n_list):
        lane = LEAF_DEV * k
        hot[CYCLE * k : CYCLE * (k + 1), :] = (
            jnp.broadcast_to(turned[:, lane : lane + 1], (CYCLE, 512)) == lon
        ).astype(BF16)
    picked = jnp.dot(hot[...], corr, preferred_element_type=F32).astype(BF16)
    start = pl.multiple_of(source * n_list, n_list)
    samples[pl.ds(start, n_list)] = picked.reshape(n_list, CYCLE, RANK)

    @pl.when(source == 0)
    def _():
        slots_down.wait()
        for part in range(2 * DEVICES // fill):
            clear(part).wait()

    for k in range(n_list):
        pltpu.make_async_copy(
            samples.at[start + k], out.at[slot_s[0, source + LEAF_DEV * k]], sem
        ).start()

    @pl.when(source == LEAF_DEV - 1)
    def _():
        pltpu.make_async_copy(samples, out.at[pl.ds(0, DEVICES)], sem).wait()


SWEEP = 32
ROUNDS = 16
PER_ROUND = 8


def exchange_kernel(
    packed, owners, transfer, gram, root,
    arrived, sums, t_ref, q_ref, p_ref, aug, first, second, part,
    send_x, recv_x, send_a, recv_a, send_b, recv_b, local, local_t,
):
    grp = lax.axis_index("grp")
    sib = lax.axis_index("sib")
    my_x, my_c = lax.div(grp, 2), lax.rem(grp, 2)
    my_y, my_z = lax.div(sib, 4), lax.rem(sib, 4)
    ys = [lax.rem(my_y + d, 4) * 4 for d in range(4)]
    zs = [lax.rem(my_z + d, 4) for d in range(4)]
    cs = [my_c, 1 - my_c]
    other = (my_x * 2 + cs[1], sib)

    def steps(lane):
        dz, dc = lane // 2 % 4, lane % 2
        return (lane // 8 + dz) % 4, dz, dc

    def sweeps(act):
        def body(sweep, carry):
            xs = [lax.rem(my_x + sweep + d, 4) * 2 for d in range(4)]
            for lane in range(SWEEP):
                dy, dz, dc = steps(lane)
                to = (xs[dy] + cs[dc], ys[dy] + zs[dz])
                if lane == 0:

                    @pl.when(sweep > 0)
                    def _():
                        act(sweep * SWEEP, to)

                else:
                    act(sweep * SWEEP + lane, to)
            return carry

        lax.fori_loop(0, 4, body, 0)

    barrier = pltpu.get_barrier_semaphore()

    def greet(k, to):
        pl.semaphore_signal(barrier, inc=1, device_id=to, device_id_type=MESH)

    sweeps(greet)
    pl.semaphore_wait(barrier, DEVICES - 1)

    def block_copy(k, to, row=0):
        return pltpu.make_async_remote_copy(
            src_ref=packed.at[row],
            dst_ref=arrived.at[k],
            send_sem=send_x.at[k],
            recv_sem=recv_x.at[k],
            device_id=to,
            device_id_type=MESH,
        )

    sweeps(lambda k, to: block_copy(k, to, to[0] * N_SIB + to[1]).start())
    own = pltpu.make_async_copy(packed.at[grp * N_SIB + sib], arrived.at[0], local)
    own.start()
    transfers_in = pltpu.make_async_copy(transfer, t_ref, local_t)
    transfers_in.start()
    sums[...] = jnp.zeros_like(sums)
    transfers_in.wait()

    def scaled(x):
        return x / jnp.max(jnp.abs(x))

    chain = scaled(t_ref[0])
    for level in range(3):
        q_ref[level] = full_dot(chain, chain, ((1,), (1,)))
        chain = full_dot(chain, t_ref[level + 1], ((1,), (0,)))
        if level < 2:
            chain = scaled(chain)
    p_ref[...] = chain
    own.wait()

    def leaves(it, lane):
        dy, dz, dc = lax.rem(lax.rem(it, 4) + lane // 2, 4), lane // 2, lane % 2
        x = lax.rem(my_x + 8 - lax.div(it, 4) - dy, 4)
        y = lax.rem(my_y + 4 - dy, 4)
        z = zs[(4 - dz) % 4]
        return owners[pl.ds((x * 2 + cs[dc]) * N_SIB + y * 4 + z, 1), :]

    def add_round(it, carry):
        @pl.when(it > 0)
        def _():
            block_copy(it * PER_ROUND, other).wait_recv()

        for lane in range(1, PER_ROUND):
            block_copy(it * PER_ROUND + lane, other).wait_recv()
        low = iota((1, 128), 1) < 64
        for half in range(2):
            start = pl.multiple_of(it * PER_ROUND, PER_ROUND) + 4 * half
            rows = arrived[pl.ds(start, 4)].reshape(4 * 2 * CYCLE, RANK)
            leaf = jnp.concatenate(
                [
                    jnp.where(low, leaves(it, 4 * half + b), leaves(it, 4 * half + b + 1))
                    for b in (0, 2)
                ],
                axis=1,
            )
            turned = rows.T
            for j in range(LEAF_DEV):
                mask = (leaf == float(j + 1)).astype(BF16)
                sums[j] = sums[j] + jnp.dot(turned * mask, rows, preferred_element_type=F32)
        return carry

    lax.fori_loop(0, ROUNDS, add_round, 0)

    eye = (iota((RANK, RANK), 0) == iota((RANK, RANK), 1)).astype(F32)

    def total(x):
        return jnp.sum(jnp.sum(x, axis=0, keepdims=True), axis=1, keepdims=True)

    whole = None
    for node in range(2):
        merged = None
        for child in range(4):
            j = 4 * node + child
            one = sums[j] * (1.0 / CYCLE) + eye
            gram[j] = one
            weighted = one * (RANK / total(one * eye))
            merged = weighted if merged is None else merged + weighted
        weighted = merged * (RANK / total(merged * q_ref[0]))
        whole = weighted if whole is None else whole + weighted
    aug[:, 0:RANK] = whole
    second_trace = total(whole * q_ref[1])
    third_trace = total(whole * q_ref[2])
    aug[:, RANK : RANK + 128] = jnp.where(
        iota((RANK, 128), 0) % 2 == 0, second_trace, third_trace
    )

    me = my_c * N_SIB + sib

    def around(act):
        for shift in range(1, TREE):
            dc, dz, dy = shift % 2, shift // 2 % 4, shift // 8
            place = (my_x * 2 + cs[dc], ys[dy] + zs[dz])
            act(shift, place, cs[dc] * N_SIB + place[1])

    def rows_copy(k, to, target):
        return pltpu.make_async_remote_copy(
            src_ref=aug.at[pl.ds(pl.multiple_of(target * 8, 8), 8), :],
            dst_ref=first.at[me],
            send_sem=send_a.at[k],
            recv_sem=recv_a.at[k],
            device_id=to,
            device_id_type=MESH,
        )

    def part_copy(k, to, target):
        return pltpu.make_async_remote_copy(
            src_ref=part,
            dst_ref=second.at[pl.ds(pl.multiple_of(me * 8, 8), 8), :],
            send_sem=send_b.at[k],
            recv_sem=recv_b.at[k],
            device_id=to,
            device_id_type=MESH,
        )

    def run(make):
        around(lambda k, to, target: make(k, to, target).start())

    def wait_rows(k, to, target):
        pltpu.make_async_remote_copy(
            src_ref=aug.at[0:8, :],
            dst_ref=first.at[source_rank(k)],
            send_sem=send_a.at[k],
            recv_sem=recv_a.at[k],
            device_id=to,
            device_id_type=MESH,
        ).wait_recv()

    def wait_part(k, to, target):
        pltpu.make_async_remote_copy(
            src_ref=part,
            dst_ref=second.at[pl.ds(pl.multiple_of(source_rank(k) * 8, 8), 8), :],
            send_sem=send_b.at[k],
            recv_sem=recv_b.at[k],
            device_id=to,
            device_id_type=MESH,
        ).wait_recv()

    def source_rank(shift):
        dc, dz, dy = shift % 2, shift // 2 % 4, shift // 8
        return cs[dc] * N_SIB + ys[(4 - dy) % 4] + zs[(4 - dz) % 4]

    def drain(make):
        around(lambda k, to, target: make(k, to, target).wait_send())

    run(rows_copy)
    first[me] = aug[pl.ds(pl.multiple_of(me * 8, 8), 8), :]
    around(wait_rows)

    gathered = None
    for quad in range(4):
        merged = None
        trace = None
        for pair in range(4):
            d = quad * 8 + pair * 2
            both = first[d] + first[d + 1]
            weight = RANK / both[0:1, RANK : RANK + 128]
            third = both[1:2, RANK : RANK + 128] * weight
            weight2 = jnp.concatenate([weight, weight], axis=1)
            scaled = both[:, 0:RANK] * weight2
            merged = scaled if merged is None else merged + scaled
            trace = third if trace is None else trace + third
        weight = RANK / trace
        scaled = merged * jnp.concatenate([weight, weight], axis=1)
        gathered = scaled if gathered is None else gathered + scaled
    part[...] = full_dot(gathered, p_ref[...], ((1,), (0,)))
    run(part_copy)
    second[pl.ds(pl.multiple_of(me * 8, 8), 8), :] = part[...]
    around(wait_part)
    root[...] = full_dot(p_ref[...], second[...], ((0,), (0,)))
    drain(rows_copy)
    drain(part_copy)

    def sent(k, carry):
        block_copy(k, other).wait_send()
        return carry

    lax.fori_loop(1, DEVICES, sent, 0)


BLOCK = 64


def factor_block(rows):
    n = rows[0].shape[0]
    sub = iota((n, 8, 128), 1)
    for r in range(len(rows)):
        scale = None
        for c in range(8):
            i = 8 * r + c
            cols = [jnp.broadcast_to(x[:, :, i : i + 1], (n, 8, 128)) for x in rows[r:]]
            s = lax.rsqrt(cols[0][:, c : c + 1, :])
            pivot = rows[r][:, c : c + 1, :] * (s * s)
            wide = jnp.broadcast_to(s, (n, 8, 128))
            scale = wide if scale is None else jnp.where(sub >= c, wide, scale)
            if c < 7:
                rows[r] = rows[r] - jnp.where(sub > c, cols[0], 0.0) * pivot
            for q in range(r + 1, len(rows)):
                rows[q] = rows[q] - cols[q - r] * pivot
        rows[r] = rows[r] * scale
    return rows


def cholesky_kernel(gram, root, leaf_out, root_out, work):
    n = LEAF_DEV + 1
    work[0:LEAF_DEV] = gram[...]
    work[LEAF_DEV] = root[...]
    lane = iota((BLOCK, 128), 1)
    eye = (lane - BLOCK == iota((BLOCK, 128), 0)).astype(F32)
    for step in range(RANK // BLOCK):
        r0 = BLOCK * step
        base = 128 * (step // 2)
        odd = step % 2
        block = work[:, r0 : r0 + BLOCK, base : base + 128]
        if odd:
            block = pltpu.roll(block, BLOCK, 2)
        block = jnp.where((lane < BLOCK)[None], block, eye[None])
        rows = factor_block([block[:, 8 * q : 8 * q + 8, :] for q in range(BLOCK // 8)])
        inverse = jnp.concatenate(rows, axis=1)
        if not odd:
            inverse = pltpu.roll(inverse, BLOCK, 2)
        inverse = jnp.where(((lane >= BLOCK) if odd else (lane < BLOCK))[None], inverse, 0.0)
        height = RANK - r0
        below = iota((height, BLOCK), 0) >= iota((height, BLOCK), 1)
        for m in range(n):
            panel = full_dot(work[m, r0:, base : base + 128], inverse[m], ((1,), (1,)))
            panel = jnp.where(below, panel, 0.0)
            out = leaf_out.at[m] if m < LEAF_DEV else root_out.at[0]
            if r0:
                out[0:r0, r0 : r0 + BLOCK] = jnp.zeros((r0, BLOCK), F32)
            out[r0:, r0 : r0 + BLOCK] = panel
            if height > BLOCK:
                c0 = 128 * ((step + 1) // 2)
                if c0 >= r0:
                    cols = panel[c0 - r0 :]
                else:
                    cols = jnp.concatenate([jnp.zeros((r0 - c0, BLOCK), F32), panel], axis=0)
                work[m, r0 + BLOCK :, c0:] = work[m, r0 + BLOCK :, c0:] - full_dot(
                    panel[BLOCK:], cols, ((1,), (1,))
                )


def sds(shape, dtype):
    return jax.ShapeDtypeStruct(shape, dtype)


def local(density, kernel, transfer, target_device, target_slot, cycle_rows):
    params = functools.partial(pltpu.CompilerParams, vmem_limit_bytes=48 * 2**20)
    packed, owners = pl.pallas_call(
        pack_kernel,
        grid=(LEAF_DEV,),
        out_shape=(sds((2 * DEVICES, CYCLE, RANK), BF16), sds((DEVICES, 128), F32)),
        in_specs=[
            pl.BlockSpec((1, 512, 512), lambda s: (s, 0, 0)),
            pl.BlockSpec((512, RANK), lambda s: (0, 0)),
            pl.BlockSpec((16, 1024), lambda s: (0, 0)),
            pl.BlockSpec((16, 1024), lambda s: (0, 0)),
            pl.BlockSpec((CYCLE, 1024), lambda s: (0, 0)),
        ],
        out_specs=(
            pl.BlockSpec(memory_space=pltpu.HBM),
            pl.BlockSpec((DEVICES, 128), lambda s: (0, 0)),
        ),
        scratch_shapes=[
            pltpu.VMEM((CYCLE, 128), F32),
            pltpu.VMEM((8, 128), I32),
            pltpu.SMEM((8, 128), I32),
            pltpu.VMEM((512, 512), BF16),
            pltpu.VMEM((DEVICES, CYCLE, RANK), BF16),
            pltpu.VMEM((32, CYCLE, RANK), BF16),
            pltpu.SemaphoreType.DMA((8,)),
            pltpu.SemaphoreType.DMA,
            pltpu.SemaphoreType.DMA,
        ],
        compiler_params=pltpu.CompilerParams(vmem_limit_bytes=62 * 2**20),
        name="pack",
    )(density, kernel, target_device.T, target_slot.T, cycle_rows.T)
    gram, root = pl.pallas_call(
        exchange_kernel,
        out_shape=(sds((LEAF_DEV, RANK, RANK), F32), sds((RANK, RANK), F32)),
        in_specs=[pl.BlockSpec(memory_space=pl.ANY), VMEM, pl.BlockSpec(memory_space=pl.ANY)],
        out_specs=(VMEM, VMEM),
        scratch_shapes=[
            pltpu.VMEM((DEVICES, 2, CYCLE, RANK), BF16),
            pltpu.VMEM((LEAF_DEV, RANK, RANK), F32),
            pltpu.VMEM((4, RANK, RANK), F32),
            pltpu.VMEM((3, RANK, RANK), F32),
            pltpu.VMEM((RANK, RANK), F32),
            pltpu.VMEM((RANK, RANK + 128), F32),
            pltpu.VMEM((TREE, 8, RANK + 128), F32),
            pltpu.VMEM((RANK, RANK), F32),
            pltpu.VMEM((8, RANK), F32),
            pltpu.SemaphoreType.DMA((DEVICES,)),
            pltpu.SemaphoreType.DMA((DEVICES,)),
            pltpu.SemaphoreType.DMA((TREE,)),
            pltpu.SemaphoreType.DMA((TREE,)),
            pltpu.SemaphoreType.DMA((TREE,)),
            pltpu.SemaphoreType.DMA((TREE,)),
            pltpu.SemaphoreType.DMA,
            pltpu.SemaphoreType.DMA,
        ],
        compiler_params=params(collective_id=1, has_side_effects=True),
        name="exchange",
    )(packed.reshape(DEVICES, 2, CYCLE, RANK), owners, transfer)
    return pl.pallas_call(
        cholesky_kernel,
        out_shape=(sds((LEAF_DEV, RANK, RANK), F32), sds((1, RANK, RANK), F32)),
        in_specs=[VMEM] * 2,
        out_specs=(VMEM, VMEM),
        scratch_shapes=[pltpu.VMEM((LEAF_DEV + 1, RANK, RANK), F32)],
        compiler_params=params(),
        name="cholesky",
    )(gram, root)


def solution(mesh):
    return jax.shard_map(
        local,
        mesh=mesh,
        in_specs=(P(("grp", "sib"), None, None), P(), P(), P(), P(), P()),
        out_specs=(P(("grp", "sib"), None, None), P(("grp", "sib"), None, None)),
        check_vma=False,
    )
```

```python
import functools

import jax
import jax.numpy as jnp
from jax import lax
from jax.experimental import pallas as pl
from jax.experimental.pallas import tpu as pltpu
from jax.sharding import PartitionSpec as P

F32 = jnp.float32
BF16 = jnp.bfloat16
I32 = jnp.int32
MESH = pl.DeviceIdType.MESH
VMEM = pl.BlockSpec(memory_space=pltpu.VMEM)

RANK = 256
LEAF_DEV = 8
CYCLE = 32
N_SIB = 16
DEVICES = 128
TREE = 32


def iota(shape, dim):
    return lax.broadcasted_iota(I32, shape, dim)


def exact_dot(a, b, dims):
    return lax.dot_general(
        a.astype(BF16), b.astype(BF16), (dims, ((), ())), preferred_element_type=F32
    )


def full_dot(a, b, dims):
    return lax.dot_general(
        a, b, (dims, ((), ())), preferred_element_type=F32, precision=lax.Precision.HIGHEST
    )


def own_device():
    return lax.axis_index("grp") * N_SIB + lax.axis_index("sib")


def pack_kernel(
    dens, kern, dev, slot, cyc, out, owners,
    picks, slot_v, slot_s, hot, samples, zeros, zero_sem, slot_sem, sem,
):
    source = pl.program_id(0)
    n_list = 16
    fill = zeros.shape[0]

    def clear(part):
        return pltpu.make_async_copy(zeros, out.at[pl.ds(part * fill, fill)], zero_sem.at[part])

    slots_down = pltpu.make_async_copy(slot_v, slot_s, slot_sem)

    @pl.when(source == 0)
    def _():
        zeros[...] = jnp.zeros_like(zeros)
        for part in range(2 * DEVICES // fill):
            clear(part).start()
        me = own_device()
        lane = iota((1024, 128), 1)
        row = iota((1024, 128), 0)
        mine = (row == me * LEAF_DEV + lane % LEAF_DEV).astype(F32)
        diagonal = iota((n_list, 128), 0) == iota((n_list, 128), 1) // LEAF_DEV

        def own_entries(x):
            wide = exact_dot(x.astype(F32), mine, ((1,), (0,)))
            return jnp.sum(jnp.where(diagonal, wide, 0.0), axis=0, keepdims=True).astype(I32)

        dest, leaf = own_entries(dev[...]), own_entries(slot[...])
        hits = (iota((DEVICES, 128), 0) == dest).astype(F32)
        earlier = (iota((128, 128), 0) % LEAF_DEV < iota((128, 128), 1) % LEAF_DEV).astype(F32)
        ahead = jnp.sum(exact_dot(hits, earlier, ((1,), (0,))) * hits, axis=0, keepdims=True)
        slot_v[...] = jnp.broadcast_to(dest * 2 + ahead.astype(I32), slot_v.shape)
        slots_down.start()
        which = (row == dest * LEAF_DEV + leaf).astype(F32)
        rows = cyc[...]
        high = exact_dot((rows // 128).astype(F32), which, ((1,), (0,)))
        low = exact_dot((rows % 128).astype(F32), which, ((1,), (0,)))
        picks[...] = high * 128.0 + low
        match = dev[...] == me
        named = jnp.sum(jnp.where(match, slot[...] + 1, 0), axis=0, keepdims=True).astype(F32)
        named = jnp.concatenate(
            [named[:, 128 * i : 128 * (i + 1)] for i in range(LEAF_DEV)], axis=0
        )
        block = jnp.logical_and(
            iota((128, 128), 0) // LEAF_DEV == iota((128, 128), 1) // LEAF_DEV,
            iota((128, 128), 0) < iota((128, 128), 1),
        )
        before = exact_dot((named > 0.5).astype(F32), block.astype(F32), ((1,), (0,)))
        here = iota((DEVICES, 128), 1) // LEAF_DEV == iota((DEVICES, 128), 0) % n_list

        def per_device(x):
            wide = jnp.broadcast_to(x[:, None, :], (LEAF_DEV, n_list, 128)).reshape(DEVICES, 128)
            return jnp.sum(jnp.where(here, wide, 0.0), axis=1, keepdims=True)

        first = per_device(jnp.where(before < 0.5, named, 0.0))
        second = per_device(jnp.where(before > 0.5, named, 0.0))
        owners[...] = jnp.where(iota((DEVICES, 128), 1) % 64 < CYCLE, first, second)

    corr = jnp.dot(dens[0], kern[...], preferred_element_type=F32).astype(BF16)
    turned = pltpu.roll(picks[...], lax.rem(128 - source, 128), 1)
    lon = iota((CYCLE, 512), 1).astype(F32)
    for k in range(n_list):
        lane = LEAF_DEV * k
        hot[CYCLE * k : CYCLE * (k + 1), :] = (
            jnp.broadcast_to(turned[:, lane : lane + 1], (CYCLE, 512)) == lon
        ).astype(BF16)
    picked = jnp.dot(hot[...], corr, preferred_element_type=F32).astype(BF16)
    start = pl.multiple_of(source * n_list, n_list)
    samples[pl.ds(start, n_list)] = picked.reshape(n_list, CYCLE, RANK)

    @pl.when(source == 0)
    def _():
        slots_down.wait()
        for part in range(2 * DEVICES // fill):
            clear(part).wait()

    for k in range(n_list):
        pltpu.make_async_copy(
            samples.at[start + k], out.at[slot_s[0, source + LEAF_DEV * k]], sem
        ).start()

    @pl.when(source == LEAF_DEV - 1)
    def _():
        pltpu.make_async_copy(samples, out.at[pl.ds(0, DEVICES)], sem).wait()


SWEEP = 32
ROUNDS = 16
PER_ROUND = 8


def exchange_kernel(
    packed, owners, transfer, gram, root,
    arrived, sums, t_ref, q_ref, p_ref, aug, first, second, part,
    send_x, recv_x, send_a, recv_a, send_b, recv_b, local, local_t,
):
    grp = lax.axis_index("grp")
    sib = lax.axis_index("sib")
    my_x, my_c = lax.div(grp, 2), lax.rem(grp, 2)
    my_y, my_z = lax.div(sib, 4), lax.rem(sib, 4)
    ys = [lax.rem(my_y + d, 4) * 4 for d in range(4)]
    zs = [lax.rem(my_z + d, 4) for d in range(4)]
    cs = [my_c, 1 - my_c]
    other = (my_x * 2 + cs[1], sib)

    def steps(lane):
        dz, dc = lane // 2 % 4, lane % 2
        return (lane // 8 + dz) % 4, dz, dc

    def sweeps(act):
        def body(sweep, carry):
            xs = [lax.rem(my_x + sweep + d, 4) * 2 for d in range(4)]
            for lane in range(SWEEP):
                dy, dz, dc = steps(lane)
                to = (xs[dy] + cs[dc], ys[dy] + zs[dz])
                if lane == 0:

                    @pl.when(sweep > 0)
                    def _():
                        act(sweep * SWEEP, to)

                else:
                    act(sweep * SWEEP + lane, to)
            return carry

        lax.fori_loop(0, 4, body, 0)

    barrier = pltpu.get_barrier_semaphore()

    def greet(k, to):
        pl.semaphore_signal(barrier, inc=1, device_id=to, device_id_type=MESH)

    sweeps(greet)
    pl.semaphore_wait(barrier, DEVICES - 1)

    def block_copy(k, to, row=0):
        return pltpu.make_async_remote_copy(
            src_ref=packed.at[row],
            dst_ref=arrived.at[k],
            send_sem=send_x.at[k],
            recv_sem=recv_x.at[k],
            device_id=to,
            device_id_type=MESH,
        )

    sweeps(lambda k, to: block_copy(k, to, to[0] * N_SIB + to[1]).start())
    own = pltpu.make_async_copy(packed.at[grp * N_SIB + sib], arrived.at[0], local)
    own.start()
    transfers_in = pltpu.make_async_copy(transfer, t_ref, local_t)
    transfers_in.start()
    sums[...] = jnp.zeros_like(sums)
    transfers_in.wait()

    def scaled(x):
        return x / jnp.max(jnp.abs(x))

    chain = scaled(t_ref[0])
    for level in range(3):
        q_ref[level] = full_dot(chain, chain, ((1,), (1,)))
        chain = full_dot(chain, t_ref[level + 1], ((1,), (0,)))
        if level < 2:
            chain = scaled(chain)
    p_ref[...] = chain
    own.wait()

    def leaves(it, lane):
        dy, dz, dc = lax.rem(lax.rem(it, 4) + lane // 2, 4), lane // 2, lane % 2
        x = lax.rem(my_x + 8 - lax.div(it, 4) - dy, 4)
        y = lax.rem(my_y + 4 - dy, 4)
        z = zs[(4 - dz) % 4]
        return owners[pl.ds((x * 2 + cs[dc]) * N_SIB + y * 4 + z, 1), :]

    def add_round(it, carry):
        @pl.when(it > 0)
        def _():
            block_copy(it * PER_ROUND, other).wait_recv()

        for lane in range(1, PER_ROUND):
            block_copy(it * PER_ROUND + lane, other).wait_recv()
        low = iota((1, 128), 1) < 64
        for half in range(2):
            start = pl.multiple_of(it * PER_ROUND, PER_ROUND) + 4 * half
            rows = arrived[pl.ds(start, 4)].reshape(4 * 2 * CYCLE, RANK)
            leaf = jnp.concatenate(
                [
                    jnp.where(low, leaves(it, 4 * half + b), leaves(it, 4 * half + b + 1))
                    for b in (0, 2)
                ],
                axis=1,
            )
            turned = rows.T
            for j in range(LEAF_DEV):
                mask = (leaf == float(j + 1)).astype(BF16)
                sums[j] = sums[j] + jnp.dot(turned * mask, rows, preferred_element_type=F32)
        return carry

    lax.fori_loop(0, ROUNDS, add_round, 0)

    eye = (iota((RANK, RANK), 0) == iota((RANK, RANK), 1)).astype(F32)

    def total(x):
        return jnp.sum(jnp.sum(x, axis=0, keepdims=True), axis=1, keepdims=True)

    whole = None
    for node in range(2):
        merged = None
        for child in range(4):
            j = 4 * node + child
            one = sums[j] * (1.0 / CYCLE) + eye
            gram[j] = one
            weighted = one * (RANK / total(one * eye))
            merged = weighted if merged is None else merged + weighted
        weighted = merged * (RANK / total(merged * q_ref[0]))
        whole = weighted if whole is None else whole + weighted
    aug[:, 0:RANK] = whole
    second_trace = total(whole * q_ref[1])
    third_trace = total(whole * q_ref[2])
    aug[:, RANK : RANK + 128] = jnp.where(
        iota((RANK, 128), 0) % 2 == 0, second_trace, third_trace
    )

    me = my_c * N_SIB + sib

    def around(act):
        for shift in range(1, TREE):
            dc, dz, dy = shift % 2, shift // 2 % 4, shift // 8
            place = (my_x * 2 + cs[dc], ys[dy] + zs[dz])
            act(shift, place, cs[dc] * N_SIB + place[1])

    def rows_copy(k, to, target):
        return pltpu.make_async_remote_copy(
            src_ref=aug.at[pl.ds(pl.multiple_of(target * 8, 8), 8), :],
            dst_ref=first.at[me],
            send_sem=send_a.at[k],
            recv_sem=recv_a.at[k],
            device_id=to,
            device_id_type=MESH,
        )

    def part_copy(k, to, target):
        return pltpu.make_async_remote_copy(
            src_ref=part,
            dst_ref=second.at[pl.ds(pl.multiple_of(me * 8, 8), 8), :],
            send_sem=send_b.at[k],
            recv_sem=recv_b.at[k],
            device_id=to,
            device_id_type=MESH,
        )

    def run(make):
        around(lambda k, to, target: make(k, to, target).start())

    def wait_rows(k, to, target):
        pltpu.make_async_remote_copy(
            src_ref=aug.at[0:8, :],
            dst_ref=first.at[source_rank(k)],
            send_sem=send_a.at[k],
            recv_sem=recv_a.at[k],
            device_id=to,
            device_id_type=MESH,
        ).wait_recv()

    def wait_part(k, to, target):
        pltpu.make_async_remote_copy(
            src_ref=part,
            dst_ref=second.at[pl.ds(pl.multiple_of(source_rank(k) * 8, 8), 8), :],
            send_sem=send_b.at[k],
            recv_sem=recv_b.at[k],
            device_id=to,
            device_id_type=MESH,
        ).wait_recv()

    def source_rank(shift):
        dc, dz, dy = shift % 2, shift // 2 % 4, shift // 8
        return cs[dc] * N_SIB + ys[(4 - dy) % 4] + zs[(4 - dz) % 4]

    def drain(make):
        around(lambda k, to, target: make(k, to, target).wait_send())

    run(rows_copy)
    first[me] = aug[pl.ds(pl.multiple_of(me * 8, 8), 8), :]
    around(wait_rows)

    gathered = None
    for quad in range(4):
        merged = None
        trace = None
        for pair in range(4):
            d = quad * 8 + pair * 2
            both = first[d] + first[d + 1]
            weight = RANK / both[0:1, RANK : RANK + 128]
            third = both[1:2, RANK : RANK + 128] * weight
            weight2 = jnp.concatenate([weight, weight], axis=1)
            scaled = both[:, 0:RANK] * weight2
            merged = scaled if merged is None else merged + scaled
            trace = third if trace is None else trace + third
        weight = RANK / trace
        scaled = merged * jnp.concatenate([weight, weight], axis=1)
        gathered = scaled if gathered is None else gathered + scaled
    part[...] = full_dot(gathered, p_ref[...], ((1,), (0,)))
    run(part_copy)
    second[pl.ds(pl.multiple_of(me * 8, 8), 8), :] = part[...]
    around(wait_part)
    root[...] = full_dot(p_ref[...], second[...], ((0,), (0,)))
    drain(rows_copy)
    drain(part_copy)

    def sent(k, carry):
        block_copy(k, other).wait_send()
        return carry

    lax.fori_loop(1, DEVICES, sent, 0)


BLOCK = 64


def factor_block(rows):
    n = rows[0].shape[0]
    sub = iota((n, 8, 128), 1)
    for r in range(len(rows)):
        scale = None
        left = len(rows) - r
        group = 4 if left <= 4 else 2
        for c0 in range(0, 8, group):
            lanes = range(8 * r + c0, 8 * r + c0 + group)
            cols = [
                [jnp.broadcast_to(x[:, :, i : i + 1], (n, 8, 128)) for x in rows[r:]]
                for i in lanes
            ]
            for a in range(group):
                c = c0 + a
                s = lax.rsqrt(cols[a][0][:, c : c + 1, :])
                inverse = s * s
                pivot = rows[r][:, c : c + 1, :] * inverse
                for later in cols[a + 1 :]:
                    share = later[0][:, c : c + 1, :] * inverse
                    for q in range(left):
                        later[q] = later[q] - cols[a][q] * share
                wide = jnp.broadcast_to(s, (n, 8, 128))
                scale = wide if scale is None else jnp.where(sub >= c, wide, scale)
                if c < 7:
                    rows[r] = rows[r] - jnp.where(sub > c, cols[a][0], 0.0) * pivot
                for q in range(1, left):
                    rows[r + q] = rows[r + q] - cols[a][q] * pivot
        rows[r] = rows[r] * scale
    return rows


def cholesky_kernel(gram, root, leaf_out, root_out, work):
    n = LEAF_DEV + 1
    work[0:LEAF_DEV] = gram[...]
    work[LEAF_DEV] = root[...]
    lane = iota((BLOCK, 128), 1)
    eye = (lane - BLOCK == iota((BLOCK, 128), 0)).astype(F32)
    for step in range(RANK // BLOCK):
        r0 = BLOCK * step
        base = 128 * (step // 2)
        odd = step % 2
        block = work[:, r0 : r0 + BLOCK, base : base + 128]
        if odd:
            block = pltpu.roll(block, BLOCK, 2)
        block = jnp.where((lane < BLOCK)[None], block, eye[None])
        rows = factor_block([block[:, 8 * q : 8 * q + 8, :] for q in range(BLOCK // 8)])
        inverse = jnp.concatenate(rows, axis=1)
        if not odd:
            inverse = pltpu.roll(inverse, BLOCK, 2)
        inverse = jnp.where(((lane >= BLOCK) if odd else (lane < BLOCK))[None], inverse, 0.0)
        height = RANK - r0
        below = iota((height, BLOCK), 0) >= iota((height, BLOCK), 1)
        for m in range(n):
            panel = full_dot(work[m, r0:, base : base + 128], inverse[m], ((1,), (1,)))
            panel = jnp.where(below, panel, 0.0)
            out = leaf_out.at[m] if m < LEAF_DEV else root_out.at[0]
            if r0:
                out[0:r0, r0 : r0 + BLOCK] = jnp.zeros((r0, BLOCK), F32)
            out[r0:, r0 : r0 + BLOCK] = panel
            if height > BLOCK:
                c0 = 128 * ((step + 1) // 2)
                if c0 >= r0:
                    cols = panel[c0 - r0 :]
                else:
                    cols = jnp.concatenate([jnp.zeros((r0 - c0, BLOCK), F32), panel], axis=0)
                work[m, r0 + BLOCK :, c0:] = work[m, r0 + BLOCK :, c0:] - full_dot(
                    panel[BLOCK:], cols, ((1,), (1,))
                )


def sds(shape, dtype):
    return jax.ShapeDtypeStruct(shape, dtype)


def local(density, kernel, transfer, target_device, target_slot, cycle_rows):
    params = functools.partial(pltpu.CompilerParams, vmem_limit_bytes=48 * 2**20)
    packed, owners = pl.pallas_call(
        pack_kernel,
        grid=(LEAF_DEV,),
        out_shape=(sds((2 * DEVICES, CYCLE, RANK), BF16), sds((DEVICES, 128), F32)),
        in_specs=[
            pl.BlockSpec((1, 512, 512), lambda s: (s, 0, 0)),
            pl.BlockSpec((512, RANK), lambda s: (0, 0)),
            pl.BlockSpec((16, 1024), lambda s: (0, 0)),
            pl.BlockSpec((16, 1024), lambda s: (0, 0)),
            pl.BlockSpec((CYCLE, 1024), lambda s: (0, 0)),
        ],
        out_specs=(
            pl.BlockSpec(memory_space=pltpu.HBM),
            pl.BlockSpec((DEVICES, 128), lambda s: (0, 0)),
        ),
        scratch_shapes=[
            pltpu.VMEM((CYCLE, 128), F32),
            pltpu.VMEM((8, 128), I32),
            pltpu.SMEM((8, 128), I32),
            pltpu.VMEM((512, 512), BF16),
            pltpu.VMEM((DEVICES, CYCLE, RANK), BF16),
            pltpu.VMEM((32, CYCLE, RANK), BF16),
            pltpu.SemaphoreType.DMA((8,)),
            pltpu.SemaphoreType.DMA,
            pltpu.SemaphoreType.DMA,
        ],
        compiler_params=pltpu.CompilerParams(vmem_limit_bytes=62 * 2**20),
        name="pack",
    )(density, kernel, target_device.T, target_slot.T, cycle_rows.T)
    gram, root = pl.pallas_call(
        exchange_kernel,
        out_shape=(sds((LEAF_DEV, RANK, RANK), F32), sds((RANK, RANK), F32)),
        in_specs=[pl.BlockSpec(memory_space=pl.ANY), VMEM, pl.BlockSpec(memory_space=pl.ANY)],
        out_specs=(VMEM, VMEM),
        scratch_shapes=[
            pltpu.VMEM((DEVICES, 2, CYCLE, RANK), BF16),
            pltpu.VMEM((LEAF_DEV, RANK, RANK), F32),
            pltpu.VMEM((4, RANK, RANK), F32),
            pltpu.VMEM((3, RANK, RANK), F32),
            pltpu.VMEM((RANK, RANK), F32),
            pltpu.VMEM((RANK, RANK + 128), F32),
            pltpu.VMEM((TREE, 8, RANK + 128), F32),
            pltpu.VMEM((RANK, RANK), F32),
            pltpu.VMEM((8, RANK), F32),
            pltpu.SemaphoreType.DMA((DEVICES,)),
            pltpu.SemaphoreType.DMA((DEVICES,)),
            pltpu.SemaphoreType.DMA((TREE,)),
            pltpu.SemaphoreType.DMA((TREE,)),
            pltpu.SemaphoreType.DMA((TREE,)),
            pltpu.SemaphoreType.DMA((TREE,)),
            pltpu.SemaphoreType.DMA,
            pltpu.SemaphoreType.DMA,
        ],
        compiler_params=params(collective_id=1, has_side_effects=True),
        name="exchange",
    )(packed.reshape(DEVICES, 2, CYCLE, RANK), owners, transfer)
    return pl.pallas_call(
        cholesky_kernel,
        out_shape=(sds((LEAF_DEV, RANK, RANK), F32), sds((1, RANK, RANK), F32)),
        in_specs=[VMEM] * 2,
        out_specs=(VMEM, VMEM),
        scratch_shapes=[pltpu.VMEM((LEAF_DEV + 1, RANK, RANK), F32)],
        compiler_params=params(),
        name="cholesky",
    )(gram, root)


def solution(mesh):
    return jax.shard_map(
        local,
        mesh=mesh,
        in_specs=(P(("grp", "sib"), None, None), P(), P(), P(), P(), P()),
        out_specs=(P(("grp", "sib"), None, None), P(("grp", "sib"), None, None)),
        check_vma=False,
    )
```

```python
import functools

import jax
import jax.numpy as jnp
from jax import lax
from jax.experimental import pallas as pl
from jax.experimental.pallas import tpu as pltpu
from jax.sharding import PartitionSpec as P

F32 = jnp.float32
BF16 = jnp.bfloat16
I32 = jnp.int32
MESH = pl.DeviceIdType.MESH
VMEM = pl.BlockSpec(memory_space=pltpu.VMEM)

RANK = 256
LEAF_DEV = 8
CYCLE = 32
N_SIB = 16
DEVICES = 128
TREE = 32


def iota(shape, dim):
    return lax.broadcasted_iota(I32, shape, dim)


def exact_dot(a, b, dims):
    return lax.dot_general(
        a.astype(BF16), b.astype(BF16), (dims, ((), ())), preferred_element_type=F32
    )


def full_dot(a, b, dims):
    return lax.dot_general(
        a, b, (dims, ((), ())), preferred_element_type=F32, precision=lax.Precision.HIGHEST
    )


def own_device():
    return lax.axis_index("grp") * N_SIB + lax.axis_index("sib")


PER_STEP = 4


def pack_kernel(
    dens, kern, dev, slot, cyc, out, owners,
    picks, slot_v, slot_s, hot, samples, zeros, zero_sem, slot_sem, sem,
):
    step = pl.program_id(0)
    n_list = 16
    fill = zeros.shape[0]

    def clear(part):
        return pltpu.make_async_copy(zeros, out.at[pl.ds(part * fill, fill)], zero_sem.at[part])

    slots_down = pltpu.make_async_copy(slot_v, slot_s, slot_sem)

    @pl.when(step == 0)
    def _():
        zeros[...] = jnp.zeros_like(zeros)
        for part in range(2 * DEVICES // fill):
            clear(part).start()
        me = own_device()
        lane = iota((1024, 128), 1)
        row = iota((1024, 128), 0)
        mine = (row == me * LEAF_DEV + lane % LEAF_DEV).astype(F32)
        diagonal = iota((n_list, 128), 0) == iota((n_list, 128), 1) // LEAF_DEV

        def own_entries(x):
            wide = exact_dot(x.astype(F32), mine, ((1,), (0,)))
            return jnp.sum(jnp.where(diagonal, wide, 0.0), axis=0, keepdims=True).astype(I32)

        dest, leaf = own_entries(dev[...]), own_entries(slot[...])
        hits = (iota((DEVICES, 128), 0) == dest).astype(F32)
        earlier = (iota((128, 128), 0) % LEAF_DEV < iota((128, 128), 1) % LEAF_DEV).astype(F32)
        ahead = jnp.sum(exact_dot(hits, earlier, ((1,), (0,))) * hits, axis=0, keepdims=True)
        slot_v[...] = jnp.broadcast_to(dest * 2 + ahead.astype(I32), slot_v.shape)
        slots_down.start()
        which = (row == dest * LEAF_DEV + leaf).astype(F32)
        rows = cyc[...]
        high = exact_dot((rows // 128).astype(F32), which, ((1,), (0,)))
        low = exact_dot((rows % 128).astype(F32), which, ((1,), (0,)))
        picks[...] = high * 128.0 + low
        match = dev[...] == me
        named = jnp.sum(jnp.where(match, slot[...] + 1, 0), axis=0, keepdims=True).astype(F32)
        named = jnp.concatenate(
            [named[:, 128 * i : 128 * (i + 1)] for i in range(LEAF_DEV)], axis=0
        )
        block = jnp.logical_and(
            iota((128, 128), 0) // LEAF_DEV == iota((128, 128), 1) // LEAF_DEV,
            iota((128, 128), 0) < iota((128, 128), 1),
        )
        before = exact_dot((named > 0.5).astype(F32), block.astype(F32), ((1,), (0,)))
        here = iota((DEVICES, 128), 1) // LEAF_DEV == iota((DEVICES, 128), 0) % n_list

        def per_device(x):
            wide = jnp.broadcast_to(x[:, None, :], (LEAF_DEV, n_list, 128)).reshape(DEVICES, 128)
            return jnp.sum(jnp.where(here, wide, 0.0), axis=1, keepdims=True)

        first = per_device(jnp.where(before < 0.5, named, 0.0))
        second = per_device(jnp.where(before > 0.5, named, 0.0))
        owners[...] = jnp.where(iota((DEVICES, 128), 1) % 64 < CYCLE, first, second)

    corr = jnp.dot(
        dens[...].reshape(PER_STEP * 512, 512), kern[...], preferred_element_type=F32
    ).astype(BF16)
    lon = iota((CYCLE, 512), 1).astype(F32)
    for sub in range(PER_STEP):
        source = step * PER_STEP + sub
        turned = pltpu.roll(picks[...], lax.rem(128 - source, 128), 1)
        for k in range(n_list):
            lane = LEAF_DEV * k
            hot[sub, CYCLE * k : CYCLE * (k + 1), :] = (
                jnp.broadcast_to(turned[:, lane : lane + 1], (CYCLE, 512)) == lon
            ).astype(BF16)
    for sub in range(PER_STEP):
        picked = jnp.dot(
            hot[sub], corr[512 * sub : 512 * (sub + 1)], preferred_element_type=F32
        ).astype(BF16)
        start = pl.multiple_of((step * PER_STEP + sub) * n_list, n_list)
        samples[pl.ds(start, n_list)] = picked.reshape(n_list, CYCLE, RANK)

    @pl.when(step == 0)
    def _():
        slots_down.wait()
        for part in range(2 * DEVICES // fill):
            clear(part).wait()

    for sub in range(PER_STEP):
        source = step * PER_STEP + sub
        for k in range(n_list):
            pltpu.make_async_copy(
                samples.at[source * n_list + k],
                out.at[slot_s[0, source + LEAF_DEV * k]],
                sem,
            ).start()

    @pl.when(step == LEAF_DEV // PER_STEP - 1)
    def _():
        pltpu.make_async_copy(samples, out.at[pl.ds(0, DEVICES)], sem).wait()


SWEEP = 32
ROUNDS = 16
PER_ROUND = 8


def exchange_kernel(
    packed, owners, transfer, gram, root,
    arrived, sums, t_ref, q_ref, p_ref, aug, first, second, part,
    send_x, recv_x, send_a, recv_a, send_b, recv_b, local, local_t,
):
    grp = lax.axis_index("grp")
    sib = lax.axis_index("sib")
    my_x, my_c = lax.div(grp, 2), lax.rem(grp, 2)
    my_y, my_z = lax.div(sib, 4), lax.rem(sib, 4)
    ys = [lax.rem(my_y + d, 4) * 4 for d in range(4)]
    zs = [lax.rem(my_z + d, 4) for d in range(4)]
    cs = [my_c, 1 - my_c]
    other = (my_x * 2 + cs[1], sib)

    def steps(lane):
        dz, dc = lane % 4, lane // 16
        return (lane // 4 + dz) % 4, dz, dc

    def sweeps(act):
        def body(sweep, carry):
            xs = [lax.rem(my_x + sweep + d, 4) * 2 for d in range(4)]
            for lane in range(SWEEP):
                dy, dz, dc = steps(lane)
                to = (xs[dy] + cs[dc], ys[dy] + zs[dz])
                if lane == 0:

                    @pl.when(sweep > 0)
                    def _():
                        act(sweep * SWEEP, to)

                else:
                    act(sweep * SWEEP + lane, to)
            return carry

        lax.fori_loop(0, 4, body, 0)

    barrier = pltpu.get_barrier_semaphore()

    def greet(k, to):
        pl.semaphore_signal(barrier, inc=1, device_id=to, device_id_type=MESH)

    sweeps(greet)
    pl.semaphore_wait(barrier, DEVICES - 1)

    def block_copy(k, to, row=0):
        return pltpu.make_async_remote_copy(
            src_ref=packed.at[row],
            dst_ref=arrived.at[k],
            send_sem=send_x.at[k],
            recv_sem=recv_x.at[k],
            device_id=to,
            device_id_type=MESH,
        )

    sweeps(lambda k, to: block_copy(k, to, to[0] * N_SIB + to[1]).start())
    own = pltpu.make_async_copy(packed.at[grp * N_SIB + sib], arrived.at[0], local)
    own.start()
    transfers_in = pltpu.make_async_copy(transfer, t_ref, local_t)
    transfers_in.start()
    sums[...] = jnp.zeros_like(sums)
    transfers_in.wait()

    def scaled(x):
        return x / jnp.max(jnp.abs(x))

    chain = scaled(t_ref[0])
    for level in range(3):
        q_ref[level] = full_dot(chain, chain, ((1,), (1,)))
        chain = full_dot(chain, t_ref[level + 1], ((1,), (0,)))
        if level < 2:
            chain = scaled(chain)
    p_ref[...] = chain
    own.wait()

    def leaves(it, lane):
        dz = lane % 4
        dy = lax.rem(lax.rem(it, 4) * 2 + lane // 4 + dz, 4)
        x = lax.rem(my_x + 8 - lax.div(it, 4) - dy, 4)
        y = lax.rem(my_y + 4 - dy, 4)
        core = lax.rem(my_c + lax.div(lax.rem(it, 4), 2), 2)
        return owners[pl.ds((x * 2 + core) * N_SIB + y * 4 + zs[(4 - dz) % 4], 1), :]

    def add_round(it, carry):
        @pl.when(it > 0)
        def _():
            block_copy(it * PER_ROUND, other).wait_recv()

        for lane in range(1, PER_ROUND):
            block_copy(it * PER_ROUND + lane, other).wait_recv()
        low = iota((1, 128), 1) < 64
        for half in range(2):
            start = pl.multiple_of(it * PER_ROUND, PER_ROUND) + 4 * half
            rows = arrived[pl.ds(start, 4)].reshape(4 * 2 * CYCLE, RANK)
            leaf = jnp.concatenate(
                [
                    jnp.where(low, leaves(it, 4 * half + b), leaves(it, 4 * half + b + 1))
                    for b in (0, 2)
                ],
                axis=1,
            )
            turned = rows.T
            for j in range(LEAF_DEV):
                mask = (leaf == float(j + 1)).astype(BF16)
                sums[j] = sums[j] + jnp.dot(turned * mask, rows, preferred_element_type=F32)
        return carry

    lax.fori_loop(0, ROUNDS, add_round, 0)

    eye = (iota((RANK, RANK), 0) == iota((RANK, RANK), 1)).astype(F32)

    def total(x):
        return jnp.sum(jnp.sum(x, axis=0, keepdims=True), axis=1, keepdims=True)

    whole = None
    for node in range(2):
        merged = None
        for child in range(4):
            j = 4 * node + child
            one = sums[j] * (1.0 / CYCLE) + eye
            gram[j] = one
            weighted = one * (RANK / total(one * eye))
            merged = weighted if merged is None else merged + weighted
        weighted = merged * (RANK / total(merged * q_ref[0]))
        whole = weighted if whole is None else whole + weighted
    aug[:, 0:RANK] = whole
    second_trace = total(whole * q_ref[1])
    third_trace = total(whole * q_ref[2])
    aug[:, RANK : RANK + 128] = jnp.where(
        iota((RANK, 128), 0) % 2 == 0, second_trace, third_trace
    )

    me = my_c * N_SIB + sib

    def around(act):
        for shift in range(1, TREE):
            dc, dz, dy = shift % 2, shift // 2 % 4, shift // 8
            place = (my_x * 2 + cs[dc], ys[dy] + zs[dz])
            act(shift, place, cs[dc] * N_SIB + place[1])

    def rows_copy(k, to, target):
        return pltpu.make_async_remote_copy(
            src_ref=aug.at[pl.ds(pl.multiple_of(target * 8, 8), 8), :],
            dst_ref=first.at[me],
            send_sem=send_a.at[k],
            recv_sem=recv_a.at[k],
            device_id=to,
            device_id_type=MESH,
        )

    def part_copy(k, to, target):
        return pltpu.make_async_remote_copy(
            src_ref=part,
            dst_ref=second.at[pl.ds(pl.multiple_of(me * 8, 8), 8), :],
            send_sem=send_b.at[k],
            recv_sem=recv_b.at[k],
            device_id=to,
            device_id_type=MESH,
        )

    def run(make):
        around(lambda k, to, target: make(k, to, target).start())

    def wait_rows(k, to, target):
        pltpu.make_async_remote_copy(
            src_ref=aug.at[0:8, :],
            dst_ref=first.at[source_rank(k)],
            send_sem=send_a.at[k],
            recv_sem=recv_a.at[k],
            device_id=to,
            device_id_type=MESH,
        ).wait_recv()

    def wait_part(k, to, target):
        pltpu.make_async_remote_copy(
            src_ref=part,
            dst_ref=second.at[pl.ds(pl.multiple_of(source_rank(k) * 8, 8), 8), :],
            send_sem=send_b.at[k],
            recv_sem=recv_b.at[k],
            device_id=to,
            device_id_type=MESH,
        ).wait_recv()

    def source_rank(shift):
        dc, dz, dy = shift % 2, shift // 2 % 4, shift // 8
        return cs[dc] * N_SIB + ys[(4 - dy) % 4] + zs[(4 - dz) % 4]

    def drain(make):
        around(lambda k, to, target: make(k, to, target).wait_send())

    run(rows_copy)
    first[me] = aug[pl.ds(pl.multiple_of(me * 8, 8), 8), :]
    around(wait_rows)

    gathered = None
    for quad in range(4):
        merged = None
        trace = None
        for pair in range(4):
            d = quad * 8 + pair * 2
            both = first[d] + first[d + 1]
            weight = RANK / both[0:1, RANK : RANK + 128]
            third = both[1:2, RANK : RANK + 128] * weight
            weight2 = jnp.concatenate([weight, weight], axis=1)
            scaled = both[:, 0:RANK] * weight2
            merged = scaled if merged is None else merged + scaled
            trace = third if trace is None else trace + third
        weight = RANK / trace
        scaled = merged * jnp.concatenate([weight, weight], axis=1)
        gathered = scaled if gathered is None else gathered + scaled
    part[...] = full_dot(gathered, p_ref[...], ((1,), (0,)))
    run(part_copy)
    second[pl.ds(pl.multiple_of(me * 8, 8), 8), :] = part[...]
    around(wait_part)
    root[...] = full_dot(p_ref[...], second[...], ((0,), (0,)))
    drain(rows_copy)
    drain(part_copy)

    def sent(k, carry):
        block_copy(k, other).wait_send()
        return carry

    lax.fori_loop(1, DEVICES, sent, 0)


BLOCK = 64


def factor_block(rows):
    n = rows[0].shape[0]
    sub = iota((n, 8, 128), 1)
    for r in range(len(rows)):
        scale = None
        left = len(rows) - r
        group = 4 if left <= 4 else 2
        for c0 in range(0, 8, group):
            lanes = range(8 * r + c0, 8 * r + c0 + group)
            cols = [
                [jnp.broadcast_to(x[:, :, i : i + 1], (n, 8, 128)) for x in rows[r:]]
                for i in lanes
            ]
            for a in range(group):
                c = c0 + a
                s = lax.rsqrt(cols[a][0][:, c : c + 1, :])
                inverse = s * s
                pivot = rows[r][:, c : c + 1, :] * inverse
                for later in cols[a + 1 :]:
                    share = later[0][:, c : c + 1, :] * inverse
                    for q in range(left):
                        later[q] = later[q] - cols[a][q] * share
                wide = jnp.broadcast_to(s, (n, 8, 128))
                scale = wide if scale is None else jnp.where(sub >= c, wide, scale)
                if c < 7:
                    rows[r] = rows[r] - jnp.where(sub > c, cols[a][0], 0.0) * pivot
                for q in range(1, left):
                    rows[r + q] = rows[r + q] - cols[a][q] * pivot
        rows[r] = rows[r] * scale
    return rows


def cholesky_kernel(gram, root, leaf_out, root_out, work):
    n = LEAF_DEV + 1
    work[0:LEAF_DEV] = gram[...]
    work[LEAF_DEV] = root[...]
    lane = iota((BLOCK, 128), 1)
    eye = (lane - BLOCK == iota((BLOCK, 128), 0)).astype(F32)
    for step in range(RANK // BLOCK):
        r0 = BLOCK * step
        base = 128 * (step // 2)
        odd = step % 2
        block = work[:, r0 : r0 + BLOCK, base : base + 128]
        if odd:
            block = pltpu.roll(block, BLOCK, 2)
        block = jnp.where((lane < BLOCK)[None], block, eye[None])
        rows = factor_block([block[:, 8 * q : 8 * q + 8, :] for q in range(BLOCK // 8)])
        inverse = jnp.concatenate(rows, axis=1)
        if not odd:
            inverse = pltpu.roll(inverse, BLOCK, 2)
        inverse = jnp.where(((lane >= BLOCK) if odd else (lane < BLOCK))[None], inverse, 0.0)
        height = RANK - r0
        below = iota((height, BLOCK), 0) >= iota((height, BLOCK), 1)
        for m in range(n):
            panel = full_dot(work[m, r0:, base : base + 128], inverse[m], ((1,), (1,)))
            panel = jnp.where(below, panel, 0.0)
            out = leaf_out.at[m] if m < LEAF_DEV else root_out.at[0]
            if r0:
                out[0:r0, r0 : r0 + BLOCK] = jnp.zeros((r0, BLOCK), F32)
            out[r0:, r0 : r0 + BLOCK] = panel
            if height > BLOCK:
                c0 = 128 * ((step + 1) // 2)
                if c0 >= r0:
                    cols = panel[c0 - r0 :]
                else:
                    cols = jnp.concatenate([jnp.zeros((r0 - c0, BLOCK), F32), panel], axis=0)
                work[m, r0 + BLOCK :, c0:] = work[m, r0 + BLOCK :, c0:] - full_dot(
                    panel[BLOCK:], cols, ((1,), (1,))
                )


def sds(shape, dtype):
    return jax.ShapeDtypeStruct(shape, dtype)


def local(density, kernel, transfer, target_device, target_slot, cycle_rows):
    params = functools.partial(pltpu.CompilerParams, vmem_limit_bytes=48 * 2**20)
    packed, owners = pl.pallas_call(
        pack_kernel,
        grid=(LEAF_DEV // PER_STEP,),
        out_shape=(sds((2 * DEVICES, CYCLE, RANK), BF16), sds((DEVICES, 128), F32)),
        in_specs=[
            pl.BlockSpec((PER_STEP, 512, 512), lambda s: (s, 0, 0)),
            pl.BlockSpec((512, RANK), lambda s: (0, 0)),
            pl.BlockSpec((16, 1024), lambda s: (0, 0)),
            pl.BlockSpec((16, 1024), lambda s: (0, 0)),
            pl.BlockSpec((CYCLE, 1024), lambda s: (0, 0)),
        ],
        out_specs=(
            pl.BlockSpec(memory_space=pltpu.HBM),
            pl.BlockSpec((DEVICES, 128), lambda s: (0, 0)),
        ),
        scratch_shapes=[
            pltpu.VMEM((CYCLE, 128), F32),
            pltpu.VMEM((8, 128), I32),
            pltpu.SMEM((8, 128), I32),
            pltpu.VMEM((PER_STEP, 512, 512), BF16),
            pltpu.VMEM((DEVICES, CYCLE, RANK), BF16),
            pltpu.VMEM((32, CYCLE, RANK), BF16),
            pltpu.SemaphoreType.DMA((8,)),
            pltpu.SemaphoreType.DMA,
            pltpu.SemaphoreType.DMA,
        ],
        compiler_params=pltpu.CompilerParams(vmem_limit_bytes=62 * 2**20),
        name="pack",
    )(density, kernel, target_device.T, target_slot.T, cycle_rows.T)
    gram, root = pl.pallas_call(
        exchange_kernel,
        out_shape=(sds((LEAF_DEV, RANK, RANK), F32), sds((RANK, RANK), F32)),
        in_specs=[pl.BlockSpec(memory_space=pl.ANY), VMEM, pl.BlockSpec(memory_space=pl.ANY)],
        out_specs=(VMEM, VMEM),
        scratch_shapes=[
            pltpu.VMEM((DEVICES, 2, CYCLE, RANK), BF16),
            pltpu.VMEM((LEAF_DEV, RANK, RANK), F32),
            pltpu.VMEM((4, RANK, RANK), F32),
            pltpu.VMEM((3, RANK, RANK), F32),
            pltpu.VMEM((RANK, RANK), F32),
            pltpu.VMEM((RANK, RANK + 128), F32),
            pltpu.VMEM((TREE, 8, RANK + 128), F32),
            pltpu.VMEM((RANK, RANK), F32),
            pltpu.VMEM((8, RANK), F32),
            pltpu.SemaphoreType.DMA((DEVICES,)),
            pltpu.SemaphoreType.DMA((DEVICES,)),
            pltpu.SemaphoreType.DMA((TREE,)),
            pltpu.SemaphoreType.DMA((TREE,)),
            pltpu.SemaphoreType.DMA((TREE,)),
            pltpu.SemaphoreType.DMA((TREE,)),
            pltpu.SemaphoreType.DMA,
            pltpu.SemaphoreType.DMA,
        ],
        compiler_params=params(collective_id=1, has_side_effects=True),
        name="exchange",
    )(packed.reshape(DEVICES, 2, CYCLE, RANK), owners, transfer)
    return pl.pallas_call(
        cholesky_kernel,
        out_shape=(sds((LEAF_DEV, RANK, RANK), F32), sds((1, RANK, RANK), F32)),
        in_specs=[VMEM] * 2,
        out_specs=(VMEM, VMEM),
        scratch_shapes=[pltpu.VMEM((LEAF_DEV + 1, RANK, RANK), F32)],
        compiler_params=params(),
        name="cholesky",
    )(gram, root)


def solution(mesh):
    return jax.shard_map(
        local,
        mesh=mesh,
        in_specs=(P(("grp", "sib"), None, None), P(), P(), P(), P(), P()),
        out_specs=(P(("grp", "sib"), None, None), P(("grp", "sib"), None, None)),
        check_vma=False,
    )
```

```python
import functools

import jax
import jax.numpy as jnp
from jax import lax
from jax.experimental import pallas as pl
from jax.experimental.pallas import tpu as pltpu
from jax.sharding import PartitionSpec as P

F32 = jnp.float32
BF16 = jnp.bfloat16
I32 = jnp.int32
MESH = pl.DeviceIdType.MESH
VMEM = pl.BlockSpec(memory_space=pltpu.VMEM)

RANK = 256
LEAF_DEV = 8
CYCLE = 32
N_SIB = 16
DEVICES = 128
TREE = 32


def iota(shape, dim):
    return lax.broadcasted_iota(I32, shape, dim)


def exact_dot(a, b, dims):
    return lax.dot_general(
        a.astype(BF16), b.astype(BF16), (dims, ((), ())), preferred_element_type=F32
    )


def full_dot(a, b, dims):
    return lax.dot_general(
        a, b, (dims, ((), ())), preferred_element_type=F32, precision=lax.Precision.HIGHEST
    )


def own_device():
    return lax.axis_index("grp") * N_SIB + lax.axis_index("sib")


PER_STEP = 4


def pack_kernel(
    dens, kern, dev, slot, cyc, out, owners,
    picks, slot_v, slot_s, hot, samples, zeros, zero_sem, slot_sem, sem,
):
    step = pl.program_id(0)
    n_list = 16
    fill = zeros.shape[0]

    def clear(part):
        return pltpu.make_async_copy(zeros, out.at[pl.ds(part * fill, fill)], zero_sem.at[part])

    slots_down = pltpu.make_async_copy(slot_v, slot_s, slot_sem)

    @pl.when(step == 0)
    def _():
        zeros[...] = jnp.zeros_like(zeros)
        for part in range(2 * DEVICES // fill):
            clear(part).start()
        me = own_device()
        lane = iota((1024, 128), 1)
        row = iota((1024, 128), 0)
        mine = (row == me * LEAF_DEV + lane % LEAF_DEV).astype(F32)
        diagonal = iota((n_list, 128), 0) == iota((n_list, 128), 1) // LEAF_DEV

        def own_entries(x):
            wide = exact_dot(x.astype(F32), mine, ((1,), (0,)))
            return jnp.sum(jnp.where(diagonal, wide, 0.0), axis=0, keepdims=True).astype(I32)

        dest, leaf = own_entries(dev[...]), own_entries(slot[...])
        hits = (iota((DEVICES, 128), 0) == dest).astype(F32)
        earlier = (iota((128, 128), 0) % LEAF_DEV < iota((128, 128), 1) % LEAF_DEV).astype(F32)
        ahead = jnp.sum(exact_dot(hits, earlier, ((1,), (0,))) * hits, axis=0, keepdims=True)
        slot_v[...] = jnp.broadcast_to(dest * 2 + ahead.astype(I32), slot_v.shape)
        slots_down.start()
        which = (row == dest * LEAF_DEV + leaf).astype(F32)
        rows = cyc[...]
        high = exact_dot((rows // 128).astype(F32), which, ((1,), (0,)))
        low = exact_dot((rows % 128).astype(F32), which, ((1,), (0,)))
        picks[...] = high * 128.0 + low
        match = dev[...] == me
        named = jnp.sum(jnp.where(match, slot[...] + 1, 0), axis=0, keepdims=True).astype(F32)
        named = jnp.concatenate(
            [named[:, 128 * i : 128 * (i + 1)] for i in range(LEAF_DEV)], axis=0
        )
        block = jnp.logical_and(
            iota((128, 128), 0) // LEAF_DEV == iota((128, 128), 1) // LEAF_DEV,
            iota((128, 128), 0) < iota((128, 128), 1),
        )
        before = exact_dot((named > 0.5).astype(F32), block.astype(F32), ((1,), (0,)))
        here = iota((DEVICES, 128), 1) // LEAF_DEV == iota((DEVICES, 128), 0) % n_list

        def per_device(x):
            wide = jnp.broadcast_to(x[:, None, :], (LEAF_DEV, n_list, 128)).reshape(DEVICES, 128)
            return jnp.sum(jnp.where(here, wide, 0.0), axis=1, keepdims=True)

        first = per_device(jnp.where(before < 0.5, named, 0.0))
        second = per_device(jnp.where(before > 0.5, named, 0.0))
        owners[...] = jnp.where(iota((DEVICES, 128), 1) % 64 < CYCLE, first, second)

    corr = jnp.dot(
        dens[...].reshape(PER_STEP * 512, 512), kern[...], preferred_element_type=F32
    ).astype(BF16)
    lon = iota((CYCLE, 512), 1).astype(F32)
    for sub in range(PER_STEP):
        source = step * PER_STEP + sub
        turned = pltpu.roll(picks[...], lax.rem(128 - source, 128), 1)
        for k in range(n_list):
            lane = LEAF_DEV * k
            hot[sub, CYCLE * k : CYCLE * (k + 1), :] = (
                jnp.broadcast_to(turned[:, lane : lane + 1], (CYCLE, 512)) == lon
            ).astype(BF16)
    for sub in range(PER_STEP):
        picked = jnp.dot(
            hot[sub], corr[512 * sub : 512 * (sub + 1)], preferred_element_type=F32
        ).astype(BF16)
        start = pl.multiple_of((step * PER_STEP + sub) * n_list, n_list)
        samples[pl.ds(start, n_list)] = picked.reshape(n_list, CYCLE, RANK)

    @pl.when(step == 0)
    def _():
        slots_down.wait()
        for part in range(2 * DEVICES // fill):
            clear(part).wait()

    for sub in range(PER_STEP):
        source = step * PER_STEP + sub
        for k in range(n_list):
            pltpu.make_async_copy(
                samples.at[source * n_list + k],
                out.at[slot_s[0, source + LEAF_DEV * k]],
                sem,
            ).start()

    @pl.when(step == LEAF_DEV // PER_STEP - 1)
    def _():
        pltpu.make_async_copy(samples, out.at[pl.ds(0, DEVICES)], sem).wait()


SWEEP = 32
ROUNDS = 16
PER_ROUND = 8


def exchange_kernel(
    packed, owners, transfer, gram, root,
    arrived, sums, t_ref, q_ref, p_ref, aug, first, second, part,
    send_x, recv_x, send_a, recv_a, send_b, recv_b, local, local_t,
):
    grp = lax.axis_index("grp")
    sib = lax.axis_index("sib")
    my_x, my_c = lax.div(grp, 2), lax.rem(grp, 2)
    my_y, my_z = lax.div(sib, 4), lax.rem(sib, 4)
    ys = [lax.rem(my_y + d, 4) * 4 for d in range(4)]
    zs = [lax.rem(my_z + d, 4) for d in range(4)]
    cs = [my_c, 1 - my_c]
    other = (my_x * 2 + cs[1], sib)

    def steps(lane):
        dz, dc = lane % 4, lane // 16
        return (lane // 4 + dz) % 4, dz, dc

    def sweeps(act):
        def body(sweep, carry):
            xs = [lax.rem(my_x + sweep + d, 4) * 2 for d in range(4)]
            for lane in range(SWEEP):
                dy, dz, dc = steps(lane)
                to = (xs[dy] + cs[dc], ys[dy] + zs[dz])
                if lane == 0:

                    @pl.when(sweep > 0)
                    def _():
                        act(sweep * SWEEP, to)

                else:
                    act(sweep * SWEEP + lane, to)
            return carry

        lax.fori_loop(0, 4, body, 0)

    barrier = pltpu.get_barrier_semaphore()

    def greet(k, to):
        pl.semaphore_signal(barrier, inc=1, device_id=to, device_id_type=MESH)

    sweeps(greet)
    pl.semaphore_wait(barrier, DEVICES - 1)

    def block_copy(k, to, row=0):
        return pltpu.make_async_remote_copy(
            src_ref=packed.at[row],
            dst_ref=arrived.at[k],
            send_sem=send_x.at[k],
            recv_sem=recv_x.at[k],
            device_id=to,
            device_id_type=MESH,
        )

    sweeps(lambda k, to: block_copy(k, to, to[0] * N_SIB + to[1]).start())
    own = pltpu.make_async_copy(packed.at[grp * N_SIB + sib], arrived.at[0], local)
    own.start()
    transfers_in = pltpu.make_async_copy(transfer, t_ref, local_t)
    transfers_in.start()
    sums[...] = jnp.zeros_like(sums)
    transfers_in.wait()

    def scaled(x):
        return x / jnp.max(jnp.abs(x))

    chain = scaled(t_ref[0])
    for level in range(3):
        q_ref[level] = full_dot(chain, chain, ((1,), (1,)))
        chain = full_dot(chain, t_ref[level + 1], ((1,), (0,)))
        if level < 2:
            chain = scaled(chain)
    p_ref[...] = chain
    own.wait()

    def leaves(it, lane):
        dz = lane % 4
        dy = lax.rem(lax.rem(it, 4) * 2 + lane // 4 + dz, 4)
        x = lax.rem(my_x + 8 - lax.div(it, 4) - dy, 4)
        y = lax.rem(my_y + 4 - dy, 4)
        core = lax.rem(my_c + lax.div(lax.rem(it, 4), 2), 2)
        return owners[pl.ds((x * 2 + core) * N_SIB + y * 4 + zs[(4 - dz) % 4], 1), :]

    def add_round(it, carry):
        @pl.when(it > 0)
        def _():
            block_copy(it * PER_ROUND, other).wait_recv()

        for lane in range(1, PER_ROUND):
            block_copy(it * PER_ROUND + lane, other).wait_recv()
        low = iota((1, 128), 1) < 64
        for half in range(2):
            start = pl.multiple_of(it * PER_ROUND, PER_ROUND) + 4 * half
            rows = arrived[pl.ds(start, 4)].reshape(4 * 2 * CYCLE, RANK)
            leaf = jnp.concatenate(
                [
                    jnp.where(low, leaves(it, 4 * half + b), leaves(it, 4 * half + b + 1))
                    for b in (0, 2)
                ],
                axis=1,
            )
            turned = rows.T
            for j in range(LEAF_DEV):
                mask = (leaf == float(j + 1)).astype(BF16)
                sums[j] = sums[j] + jnp.dot(turned * mask, rows, preferred_element_type=F32)
        return carry

    lax.fori_loop(0, ROUNDS, add_round, 0)

    eye = (iota((RANK, RANK), 0) == iota((RANK, RANK), 1)).astype(F32)

    def total(x):
        return jnp.sum(jnp.sum(x, axis=0, keepdims=True), axis=1, keepdims=True)

    whole = None
    for node in range(2):
        merged = None
        for child in range(4):
            j = 4 * node + child
            one = sums[j] * (1.0 / CYCLE) + eye
            gram[j] = one
            weighted = one * (RANK / total(one * eye))
            merged = weighted if merged is None else merged + weighted
        weighted = merged * (RANK / total(merged * q_ref[0]))
        whole = weighted if whole is None else whole + weighted
    aug[:, 0:RANK] = whole
    second_trace = total(whole * q_ref[1])
    third_trace = total(whole * q_ref[2])
    aug[:, RANK : RANK + 128] = jnp.where(
        iota((RANK, 128), 0) % 2 == 0, second_trace, third_trace
    )

    me = my_c * N_SIB + sib

    def around(act):
        for shift in range(1, TREE):
            dc, dz, dy = shift // 16, shift % 4, (shift // 4 + shift) % 4
            place = (my_x * 2 + cs[dc], ys[dy] + zs[dz])
            act(shift, place, cs[dc] * N_SIB + place[1])

    def rows_copy(k, to, target):
        return pltpu.make_async_remote_copy(
            src_ref=aug.at[pl.ds(pl.multiple_of(target * 8, 8), 8), :],
            dst_ref=first.at[me],
            send_sem=send_a.at[k],
            recv_sem=recv_a.at[k],
            device_id=to,
            device_id_type=MESH,
        )

    def part_copy(k, to, target):
        return pltpu.make_async_remote_copy(
            src_ref=part,
            dst_ref=second.at[pl.ds(pl.multiple_of(me * 8, 8), 8), :],
            send_sem=send_b.at[k],
            recv_sem=recv_b.at[k],
            device_id=to,
            device_id_type=MESH,
        )

    def run(make):
        around(lambda k, to, target: make(k, to, target).start())

    def wait_rows(k, to, target):
        pltpu.make_async_remote_copy(
            src_ref=aug.at[0:8, :],
            dst_ref=first.at[source_rank(k)],
            send_sem=send_a.at[k],
            recv_sem=recv_a.at[k],
            device_id=to,
            device_id_type=MESH,
        ).wait_recv()

    def wait_part(k, to, target):
        pltpu.make_async_remote_copy(
            src_ref=part,
            dst_ref=second.at[pl.ds(pl.multiple_of(source_rank(k) * 8, 8), 8), :],
            send_sem=send_b.at[k],
            recv_sem=recv_b.at[k],
            device_id=to,
            device_id_type=MESH,
        ).wait_recv()

    def source_rank(shift):
        dc, dz, dy = shift // 16, shift % 4, (shift // 4 + shift) % 4
        return cs[dc] * N_SIB + ys[(4 - dy) % 4] + zs[(4 - dz) % 4]

    def drain(make):
        around(lambda k, to, target: make(k, to, target).wait_send())

    run(rows_copy)
    first[me] = aug[pl.ds(pl.multiple_of(me * 8, 8), 8), :]
    around(wait_rows)

    gathered = None
    for quad in range(4):
        merged = None
        trace = None
        for pair in range(4):
            d = quad * 8 + pair * 2
            both = first[d] + first[d + 1]
            weight = RANK / both[0:1, RANK : RANK + 128]
            third = both[1:2, RANK : RANK + 128] * weight
            weight2 = jnp.concatenate([weight, weight], axis=1)
            scaled = both[:, 0:RANK] * weight2
            merged = scaled if merged is None else merged + scaled
            trace = third if trace is None else trace + third
        weight = RANK / trace
        scaled = merged * jnp.concatenate([weight, weight], axis=1)
        gathered = scaled if gathered is None else gathered + scaled
    part[...] = full_dot(gathered, p_ref[...], ((1,), (0,)))
    run(part_copy)
    second[pl.ds(pl.multiple_of(me * 8, 8), 8), :] = part[...]
    around(wait_part)
    root[...] = full_dot(p_ref[...], second[...], ((0,), (0,)))
    drain(rows_copy)
    drain(part_copy)

    def sent(k, carry):
        block_copy(k, other).wait_send()
        return carry

    lax.fori_loop(1, DEVICES, sent, 0)


BLOCK = 64


def factor_block(rows):
    n = rows[0].shape[0]
    sub = iota((n, 8, 128), 1)
    for r in range(len(rows)):
        scale = None
        left = len(rows) - r
        group = 4 if left <= 4 else 2
        for c0 in range(0, 8, group):
            lanes = range(8 * r + c0, 8 * r + c0 + group)
            cols = [
                [jnp.broadcast_to(x[:, :, i : i + 1], (n, 8, 128)) for x in rows[r:]]
                for i in lanes
            ]
            for a in range(group):
                c = c0 + a
                s = lax.rsqrt(cols[a][0][:, c : c + 1, :])
                inverse = s * s
                pivot = rows[r][:, c : c + 1, :] * inverse
                for later in cols[a + 1 :]:
                    share = later[0][:, c : c + 1, :] * inverse
                    for q in range(left):
                        later[q] = later[q] - cols[a][q] * share
                wide = jnp.broadcast_to(s, (n, 8, 128))
                scale = wide if scale is None else jnp.where(sub >= c, wide, scale)
                if c < 7:
                    rows[r] = rows[r] - jnp.where(sub > c, cols[a][0], 0.0) * pivot
                for q in range(1, left):
                    rows[r + q] = rows[r + q] - cols[a][q] * pivot
        rows[r] = rows[r] * scale
    return rows


def cholesky_kernel(gram, root, leaf_out, root_out, work):
    n = LEAF_DEV + 1
    work[0:LEAF_DEV] = gram[...]
    work[LEAF_DEV] = root[...]
    lane = iota((BLOCK, 128), 1)
    eye = (lane - BLOCK == iota((BLOCK, 128), 0)).astype(F32)
    for step in range(RANK // BLOCK):
        r0 = BLOCK * step
        base = 128 * (step // 2)
        odd = step % 2
        block = work[:, r0 : r0 + BLOCK, base : base + 128]
        if odd:
            block = pltpu.roll(block, BLOCK, 2)
        block = jnp.where((lane < BLOCK)[None], block, eye[None])
        rows = factor_block([block[:, 8 * q : 8 * q + 8, :] for q in range(BLOCK // 8)])
        inverse = jnp.concatenate(rows, axis=1)
        if not odd:
            inverse = pltpu.roll(inverse, BLOCK, 2)
        inverse = jnp.where(((lane >= BLOCK) if odd else (lane < BLOCK))[None], inverse, 0.0)
        height = RANK - r0
        below = iota((height, BLOCK), 0) >= iota((height, BLOCK), 1)
        for m in range(n):
            panel = full_dot(work[m, r0:, base : base + 128], inverse[m], ((1,), (1,)))
            panel = jnp.where(below, panel, 0.0)
            out = leaf_out.at[m] if m < LEAF_DEV else root_out.at[0]
            if r0:
                out[0:r0, r0 : r0 + BLOCK] = jnp.zeros((r0, BLOCK), F32)
            out[r0:, r0 : r0 + BLOCK] = panel
            if height > BLOCK:
                c0 = 128 * ((step + 1) // 2)
                if c0 >= r0:
                    cols = panel[c0 - r0 :]
                else:
                    cols = jnp.concatenate([jnp.zeros((r0 - c0, BLOCK), F32), panel], axis=0)
                work[m, r0 + BLOCK :, c0:] = work[m, r0 + BLOCK :, c0:] - full_dot(
                    panel[BLOCK:], cols, ((1,), (1,))
                )


def sds(shape, dtype):
    return jax.ShapeDtypeStruct(shape, dtype)


def local(density, kernel, transfer, target_device, target_slot, cycle_rows):
    params = functools.partial(pltpu.CompilerParams, vmem_limit_bytes=48 * 2**20)
    packed, owners = pl.pallas_call(
        pack_kernel,
        grid=(LEAF_DEV // PER_STEP,),
        out_shape=(sds((2 * DEVICES, CYCLE, RANK), BF16), sds((DEVICES, 128), F32)),
        in_specs=[
            pl.BlockSpec((PER_STEP, 512, 512), lambda s: (s, 0, 0)),
            pl.BlockSpec((512, RANK), lambda s: (0, 0)),
            pl.BlockSpec((16, 1024), lambda s: (0, 0)),
            pl.BlockSpec((16, 1024), lambda s: (0, 0)),
            pl.BlockSpec((CYCLE, 1024), lambda s: (0, 0)),
        ],
        out_specs=(
            pl.BlockSpec(memory_space=pltpu.HBM),
            pl.BlockSpec((DEVICES, 128), lambda s: (0, 0)),
        ),
        scratch_shapes=[
            pltpu.VMEM((CYCLE, 128), F32),
            pltpu.VMEM((8, 128), I32),
            pltpu.SMEM((8, 128), I32),
            pltpu.VMEM((PER_STEP, 512, 512), BF16),
            pltpu.VMEM((DEVICES, CYCLE, RANK), BF16),
            pltpu.VMEM((32, CYCLE, RANK), BF16),
            pltpu.SemaphoreType.DMA((8,)),
            pltpu.SemaphoreType.DMA,
            pltpu.SemaphoreType.DMA,
        ],
        compiler_params=pltpu.CompilerParams(vmem_limit_bytes=62 * 2**20),
        name="pack",
    )(density, kernel, target_device.T, target_slot.T, cycle_rows.T)
    gram, root = pl.pallas_call(
        exchange_kernel,
        out_shape=(sds((LEAF_DEV, RANK, RANK), F32), sds((RANK, RANK), F32)),
        in_specs=[pl.BlockSpec(memory_space=pl.ANY), VMEM, pl.BlockSpec(memory_space=pl.ANY)],
        out_specs=(VMEM, VMEM),
        scratch_shapes=[
            pltpu.VMEM((DEVICES, 2, CYCLE, RANK), BF16),
            pltpu.VMEM((LEAF_DEV, RANK, RANK), F32),
            pltpu.VMEM((4, RANK, RANK), F32),
            pltpu.VMEM((3, RANK, RANK), F32),
            pltpu.VMEM((RANK, RANK), F32),
            pltpu.VMEM((RANK, RANK + 128), F32),
            pltpu.VMEM((TREE, 8, RANK + 128), F32),
            pltpu.VMEM((RANK, RANK), F32),
            pltpu.VMEM((8, RANK), F32),
            pltpu.SemaphoreType.DMA((DEVICES,)),
            pltpu.SemaphoreType.DMA((DEVICES,)),
            pltpu.SemaphoreType.DMA((TREE,)),
            pltpu.SemaphoreType.DMA((TREE,)),
            pltpu.SemaphoreType.DMA((TREE,)),
            pltpu.SemaphoreType.DMA((TREE,)),
            pltpu.SemaphoreType.DMA,
            pltpu.SemaphoreType.DMA,
        ],
        compiler_params=params(collective_id=1, has_side_effects=True),
        name="exchange",
    )(packed.reshape(DEVICES, 2, CYCLE, RANK), owners, transfer)
    return pl.pallas_call(
        cholesky_kernel,
        out_shape=(sds((LEAF_DEV, RANK, RANK), F32), sds((1, RANK, RANK), F32)),
        in_specs=[VMEM] * 2,
        out_specs=(VMEM, VMEM),
        scratch_shapes=[pltpu.VMEM((LEAF_DEV + 1, RANK, RANK), F32)],
        compiler_params=params(),
        name="cholesky",
    )(gram, root)


def solution(mesh):
    return jax.shard_map(
        local,
        mesh=mesh,
        in_specs=(P(("grp", "sib"), None, None), P(), P(), P(), P(), P()),
        out_specs=(P(("grp", "sib"), None, None), P(("grp", "sib"), None, None)),
        check_vma=False,
    )
```
